32 devices in a mesh: expert: 8 (over y, x, core), tensor: 4 (over z).
Axes of the slice: x: 2, y: 2, z: 4, core: 2. Of those that a mesh axis runs over, the one named last changes fastest.
Arguments:
- inputs: bfloat16 [16384, 1024], P(('expert', 'tensor')), may hold values from -6 to 6
- gain_one: float32 [1024], replicated, may hold values from 0.5 to 1.5
- w_query: bfloat16 [1024, 1024], P(None, 'tensor'), may hold values from -0.1875 to 0.1875
- w_key: bfloat16 [1024, 1024], P(None, 'tensor'), may hold values from -0.1875 to 0.1875
- w_value: bfloat16 [1024, 1024], P(None, 'tensor'), may hold values from -0.1875 to 0.1875
- w_out: bfloat16 [1024, 1024], P('tensor'), may hold values from -1.5 to 1.5
- rel_table: float32 [32, 16], P(None, 'tensor'), may hold values from -4 to 4
- gain_two: float32 [1024], replicated, may hold values from 0.5 to 1.5
- router: float32 [1024, 32], replicated, may hold values from -0.125 to 0.125
- w_gate: bfloat16 [32, 1024, 2816], P('expert', None, 'tensor'), may hold values from -0.1875 to 0.1875
- w_up: bfloat16 [32, 1024, 2816], P('expert', None, 'tensor'), may hold values from -0.1875 to 0.1875
- w_down: bfloat16 [32, 2816, 1024], P('expert', 'tensor'), may hold values from -0.15625 to 0.15625
- routes: int32 [16384, 2], replicated, may hold values from 0 to 31, as said below
- buckets: int32 [512, 512], replicated, may hold values from 0 to 31
- grad_out: bfloat16 [16384, 1024], P(('expert', 'tensor')), may hold values from -6 to 6
Outputs:
- output: bfloat16 [16384, 1024], P(('expert', 'tensor'))
- input_grad: float32 [16384, 1024], P(('expert', 'tensor'))
- gain_one_grad: float32 [1024], replicated
- query_grad: float32 [1024, 1024], P(None, 'tensor')
- key_grad: float32 [1024, 1024], P(None, 'tensor')
- value_grad: float32 [1024, 1024], P(None, 'tensor')
- out_proj_grad: float32 [1024, 1024], P('tensor')
- table_grad: float32 [32, 16], P(None, 'tensor')
- gain_two_grad: float32 [1024], replicated
- router_grad: float32 [1024, 32], replicated
- gate_grad: float32 [32, 1024, 2816], P('expert', None, 'tensor')
- up_grad: float32 [32, 1024, 2816], P('expert', None, 'tensor')
- down_grad: float32 [32, 2816, 1024], P('expert', 'tensor')
- aux_losses: float32 [2], replicated
The draws below stay inside these ranges and needn't reach their ends.
Inputs may be any that keep to these rules, and one draw needn't show every extreme that they name: `routes`: each row names two different experts. Within the tokens of one device a few experts are named far more often than the mean, and which ones changes from device to device.
All inputs are finite; a program needn't handle non-finite values.
Results may differ from the reference program's by a relative error of at most 0.023.
Values may be sent and summed in bfloat16 or wider, within the bound.
No kernel may reach another device: no remote copies, remote signals or barrier semaphores. Data moves between devices by JAX's collectives and lax.ppermute only.
A program may use at most 320 MiB of HBM per device.

```python
import jax
import jax.numpy as jnp
from jax import lax

D = 1024
HEADS = 16
HEAD_DIM = 64
FF = 2816
EXPERTS = 32
BUCKETS = 32
TOP = 2
SEQ = 512
TOK_DEV = 512
TOKENS = 16384
CAP = 40
N_EXPERT = 8
N_TENSOR = 4


def draw_routes(key, part):
    key = jax.random.fold_in(key, 11)
    first_key, second_key = jax.random.split(key, 2)
    tries = jax.random.randint(first_key, (TOKENS, 3), 0, EXPERTS)
    favored = jnp.min(tries, axis=1)
    drift = jnp.arange(TOKENS, dtype=jnp.int32) // TOK_DEV * 5
    first_choice = (favored + drift) % EXPERTS
    stride = jax.random.randint(second_key, (TOKENS,), 1, EXPERTS)
    second_choice = (first_choice + stride) % EXPERTS
    return jnp.stack([first_choice, second_choice], 1).astype(jnp.int32)


def set_ends(drawn, own_key, least, top_value):
    shape = drawn.shape
    place = [jax.random.randint(jax.random.fold_in(own_key, axis), (), 0, shape[axis]) for axis in range(len(shape))]
    drawn = drawn.at[tuple(place)].set(least)
    longest = shape.index(max(shape))
    place[longest] = (place[longest] + 1) % shape[longest]
    return drawn.at[tuple(place)].set(top_value)


def block_scale(stream_key, dims, shards, smallest, largest):
    def one(axis_at, shards_of):
        draws = jax.random.uniform(jax.random.fold_in(jax.random.fold_in(stream_key, 6), axis_at), (shards_of,), jnp.float32, smallest / len(shards), largest / len(shards))
        return jnp.repeat(jnp.exp(draws), dims[axis_at] // shards_of).reshape((-1,) + (1,) * (len(dims) - axis_at - 1))

    level = one(*shards[0])
    for cut in shards[1:]:
        level = level * one(*cut)
    return level


def gaussian(own_key, dims, spread, limit, cuts=(), held_as=jnp.bfloat16):
    values = jax.random.normal(own_key, dims, jnp.float32) * spread
    if len(cuts) > 0:
        values = block_scale(own_key, dims, cuts, -0.22, 0.18) * values
    return jnp.clip(values, min=-limit, max=limit).astype(held_as)


def setup_inputs(seed: int = 0) -> dict:
    seeds = jax.random.split(jax.random.key(seed), 16)
    inputs = gaussian(seeds[0], (TOKENS, D), 1.0, 6.0, ((0, 32),))
    gain_one = jnp.clip(1.0 + 0.1 * jax.random.normal(seeds[1], (D,), jnp.float32), 0.5, 1.5)
    w_query = gaussian(seeds[2], (D, D), D ** -0.5, 0.1875, ((1, 4),))
    w_key = gaussian(seeds[3], (D, D), D ** -0.5, 0.1875, ((1, 4),))
    w_value = gaussian(seeds[4], (D, D), D ** -0.5, 0.1875, ((1, 4),))
    w_out = gaussian(seeds[5], (D, D), (D // 64) ** -0.5, 1.5, ((0, 4),))
    rel_table = gaussian(seeds[6], (BUCKETS, HEADS), 1.0, 4.0, ((1, 4),), jnp.float32)
    gain_two = jnp.clip(1.0 + 0.1 * jax.random.normal(seeds[7], (D,), jnp.float32), 0.5, 1.5)
    router = gaussian(seeds[8], (D, EXPERTS), (2 * D) ** -0.5, 0.125, (), jnp.float32)
    w_gate = gaussian(seeds[9], (EXPERTS, D, FF), D ** -0.5, 0.1875, ((0, 8), (2, 4)))
    w_up = gaussian(seeds[10], (EXPERTS, D, FF), D ** -0.5, 0.1875, ((0, 8), (2, 4)))
    w_down = gaussian(seeds[11], (EXPERTS, FF, D), (FF // 2) ** -0.5, 0.15625, ((0, 8), (1, 4)))
    routes = draw_routes(jax.random.fold_in(seeds[15], 71), 0)
    buckets = set_ends(jax.random.randint(seeds[13], (SEQ, SEQ), 0, BUCKETS), jax.random.fold_in(seeds[13], 1), 0, BUCKETS - 1).astype(jnp.int32)
    grad_out = gaussian(seeds[14], (TOKENS, D), 1.0, 6.0, ((0, 32),))
    return {"inputs": inputs, "gain_one": gain_one, "w_query": w_query, "w_key": w_key, "w_value": w_value, "w_out": w_out, "rel_table": rel_table, "gain_two": gain_two, "router": router, "w_gate": w_gate, "w_up": w_up, "w_down": w_down, "routes": routes, "buckets": buckets, "grad_out": grad_out}


epsilon = 1e-06
balance_weight = 0.01
zloss_weight = 0.001
highest = lax.Precision.HIGHEST

@jax.custom_vjp
def low(v):
    return lax.optimization_barrier(v.astype(jnp.bfloat16)).astype(jnp.float32)

@jax.custom_vjp
def low_back(v):
    return v

def low_keep(v):
    return (low(v), None)

def low_pass(kept, grad):
    return (grad,)

def back_keep(v):
    return (v, None)

def back_low(kept, grad):
    return (low(grad),)
low.defvjp(low_keep, low_pass)
low_back.defvjp(back_keep, back_low)

def both_ways(value):
    return low_back(low(value))

def rms_scale(rows_in, gain):
    inverse = lax.rsqrt(lax.optimization_barrier(jnp.mean(rows_in * rows_in, axis=-1, keepdims=True)) + epsilon)
    return rows_in * inverse * gain

def slot_index(routes):
    devices = N_EXPERT * N_TENSOR
    grouped = routes.reshape(devices, TOK_DEV, TOP)
    labels = jnp.arange(EXPERTS, dtype=jnp.int32)

    def one_group(group_routes, device):
        marks = (group_routes[:, :, None] == labels).astype(jnp.int32)
        first_pick = marks[:, 0]
        second_pick = marks[:, 1]
        ahead_one = jnp.cumsum(first_pick, 0) - first_pick
        ahead_two = lax.optimization_barrier(jnp.sum(first_pick, 0)) + jnp.cumsum(second_pick, 0) - second_pick
        places = jnp.stack([lax.optimization_barrier(jnp.sum(ahead_one * first_pick, -1)), lax.optimization_barrier(jnp.sum(ahead_two * second_pick, -1))], 1)
        target = group_routes * (devices * CAP) + device * CAP + places
        return jnp.where(places < CAP, target, EXPERTS * devices * CAP).astype(jnp.int32)
    return jax.vmap(one_group)(grouped, jnp.arange(devices, dtype=jnp.int32)).reshape(-1, TOP)

def forward(inputs_f, gain_one, w_query, w_key, w_value, w_out, rel_table, gain_two, router, w_gate, w_up, w_down, routes, buckets):
    tokens = inputs_f.shape[0]
    normed_one = low(rms_scale(inputs_f, gain_one))
    queries = both_ways(jnp.dot(normed_one, w_query, precision=highest))
    key_rows = both_ways(jnp.dot(normed_one, w_key, precision=highest))
    val_rows = both_ways(jnp.dot(normed_one, w_value, precision=highest))
    seq_shape = (tokens // SEQ, SEQ, HEADS, HEAD_DIM)
    pos_bias = jnp.transpose(rel_table[buckets], (2, 0, 1))

    def attend(triple):
        query_seq, key_seq, val_seq = triple
        scores = jnp.einsum('qhd,khd->hqk', query_seq, key_seq, precision=highest) * 0.125 + pos_bias
        scores = low_back(scores)
        weights = jax.nn.softmax(scores, axis=-1)
        return jnp.einsum('hqk,khd->qhd', low(weights), val_seq, precision=highest)
    attended = lax.map(jax.checkpoint(attend), (queries.reshape(seq_shape), key_rows.reshape(seq_shape), val_rows.reshape(seq_shape)))
    attended = both_ways(attended.reshape(tokens, D))
    attn_out = low_back(jnp.dot(attended, w_out, precision=highest))
    resid = inputs_f + attn_out
    normed_two = rms_scale(resid, gain_two)
    logits = jnp.dot(normed_two, router, precision=highest)
    router_probs = jax.nn.softmax(logits, axis=-1)
    log_totals = jax.nn.logsumexp(logits, axis=-1)
    zloss = jnp.mean(log_totals * log_totals)
    counts = lax.optimization_barrier(jnp.sum((routes[:, :, None] == jnp.arange(EXPERTS, dtype=jnp.int32)).astype(jnp.float32), axis=(0, 1)))
    route_share = counts / (tokens * TOP)
    balance = EXPERTS * jnp.sum(route_share * lax.optimization_barrier(jnp.mean(router_probs, axis=0)))
    chosen = jnp.take_along_axis(router_probs, routes, axis=1)
    gate_weights = chosen / lax.optimization_barrier(jnp.sum(chosen, axis=-1, keepdims=True))
    flat_index = slot_index(routes)
    total_slots = EXPERTS * N_EXPERT * N_TENSOR * CAP
    sent = low(normed_two)
    buffer = jnp.zeros((total_slots + 1, D), jnp.float32).at[flat_index].add(jnp.broadcast_to(sent[:, None, :], (tokens, TOP, D)))
    buffer = low_back(buffer[:total_slots].reshape(EXPERTS, total_slots // EXPERTS, D))

    def expert(quad):
        slot_rows, gate_w, up_w, down_w = quad
        gate_val = low_back(jnp.dot(slot_rows, gate_w, precision=highest))
        up_val = low_back(jnp.dot(slot_rows, up_w, precision=highest))
        hidden = low(jax.nn.gelu(gate_val, approximate=True) * up_val)
        return both_ways(jnp.dot(hidden, down_w, precision=highest))
    returned = lax.map(jax.checkpoint(expert), (buffer, w_gate, w_up, w_down))
    returned = jnp.concatenate([returned.reshape(total_slots, D), jnp.zeros((1, D), jnp.float32)], 0)
    picked = returned[flat_index]
    mixture = gate_weights[:, 0:1] * picked[:, 0] + gate_weights[:, 1:2] * picked[:, 1]
    return (resid + mixture, jnp.stack([balance, zloss]))

def reference(inputs, gain_one, w_query, w_key, w_value, w_out, rel_table, gain_two, router, w_gate, w_up, w_down, routes, buckets, grad_out):

    def closed(inputs_f, gain_a, query_w, key_w, value_w, out_w, table_w, gain_b, router_w, gate_w, up_w, down_w):
        return forward(inputs_f, gain_a, query_w, key_w, value_w, out_w, table_w, gain_b, router_w, gate_w, up_w, down_w, routes, buckets)
    results, pullback = jax.vjp(closed, inputs.astype(jnp.float32), gain_one, w_query.astype(jnp.float32), w_key.astype(jnp.float32), w_value.astype(jnp.float32), w_out.astype(jnp.float32), rel_table, gain_two, router, w_gate.astype(jnp.float32), w_up.astype(jnp.float32), w_down.astype(jnp.float32))
    output_f, losses = results
    grads = pullback((grad_out.astype(jnp.float32), jnp.array([balance_weight, zloss_weight], jnp.float32)))
    return (output_f.astype(jnp.bfloat16), grads[0], grads[1], grads[2], grads[3], grads[4], grads[5], grads[6], grads[7], grads[8], grads[9], grads[10], grads[11], losses)
```

```python
import functools

import jax
import jax.numpy as jnp
from jax import lax
from jax.experimental import pallas as pl
from jax.experimental.pallas import tpu as pltpu
from jax.sharding import PartitionSpec as P

HEAD_DIM = 64
TOP = 2
LANES = 128
MIB = 2**20

epsilon = 1e-06
balance_weight = 0.01
zloss_weight = 0.001
highest = lax.Precision.HIGHEST

BF = jnp.bfloat16
F32 = jnp.float32
NN = (((1,), (0,)), ((), ()))
NT = (((1,), (1,)), ((), ()))
TN = (((0,), (0,)), ((), ()))


def dot(left, right, dims=NN):
    return lax.dot_general(left, right, dims, preferred_element_type=F32)


def rms_scale(rows_in, gain):
    inverse = lax.rsqrt(jnp.mean(rows_in * rows_in, axis=-1, keepdims=True) + epsilon)
    return rows_in * inverse * gain


def lookup(row, index):
    table = jnp.broadcast_to(row, (index.shape[0], LANES))
    parts = [
        jnp.take_along_axis(table, index[:, at : at + LANES], axis=1)
        for at in range(0, index.shape[1], LANES)
    ]
    return jnp.concatenate(parts, axis=1)


def attend_kernel(q_ref, k_ref, v_ref, bucket_ref, table_ref, out_ref, prob_ref, *, tile):
    low = lax.broadcasted_iota(jnp.int32, (tile, LANES), 1) < HEAD_DIM
    for start in range(0, q_ref.shape[0], tile):
        rows = pl.ds(start, tile)
        query = q_ref[rows, :]
        mixed = []
        for head in range(2):
            part = jnp.where(low if head == 0 else ~low, query, jnp.zeros_like(query))
            scores = dot(part, k_ref[...], NT) * 0.125 + lookup(
                table_ref[0, head : head + 1, :], bucket_ref[rows, :]
            )
            scores = jnp.exp(scores - jnp.max(scores, axis=-1, keepdims=True))
            weights = (scores / jnp.sum(scores, axis=-1, keepdims=True)).astype(BF)
            prob_ref[head, rows, :] = weights
            mixed.append(dot(weights, v_ref[...]))
        out_ref[rows, :] = jnp.where(low, mixed[0], mixed[1]).astype(BF)


def attend(qkv, buckets, table):
    seq, cols = qkv.shape
    pairs = cols // (3 * LANES)

    def col(part):
        return pl.BlockSpec((seq, LANES), lambda p: (0, part * pairs + p))

    return pl.pallas_call(
        functools.partial(attend_kernel, tile=128),
        grid=(pairs,),
        in_specs=[
            col(0),
            col(1),
            col(2),
            pl.BlockSpec((seq, seq), lambda p: (0, 0)),
            pl.BlockSpec((1, 2, LANES), lambda p: (p, 0, 0)),
        ],
        out_specs=[col(0), pl.BlockSpec((2, seq, seq), lambda p: (p, 0, 0))],
        out_shape=[
            jax.ShapeDtypeStruct((seq, pairs * LANES), BF),
            jax.ShapeDtypeStruct((2 * pairs, seq, seq), BF),
        ],
        compiler_params=pltpu.CompilerParams(vmem_limit_bytes=40 * MIB),
        name="attend",
    )(qkv, qkv, qkv, buckets, table)


def attend_back_kernel(
    q_ref, k_ref, v_ref, grad_ref, prob_ref, dq_ref, dk_ref, dv_ref, score_ref, *, tile
):
    seq = q_ref.shape[0]
    low = lax.broadcasted_iota(jnp.int32, (tile, LANES), 1) < HEAD_DIM
    for start in range(0, seq, tile):
        rows = pl.ds(start, tile)
        grad = grad_ref[rows, :]
        back = []
        for head in range(2):
            part = jnp.where(low if head == 0 else ~low, grad, jnp.zeros_like(grad))
            weights = prob_ref[head, rows, :].astype(F32)
            weight_grad = dot(part, v_ref[...], NT)
            score = weights * (
                weight_grad - jnp.sum(weights * weight_grad, axis=-1, keepdims=True)
            )
            score = score.astype(BF)
            score_ref[head, rows, :] = score
            back.append(dot(score, k_ref[...]))
        dq_ref[rows, :] = (jnp.where(low, back[0], back[1]) * 0.125).astype(BF)
    wide = lax.broadcasted_iota(jnp.int32, (seq, LANES), 1) < HEAD_DIM
    keys = [dot(score_ref[head], q_ref[...], TN) for head in range(2)]
    dk_ref[...] = (jnp.where(wide, keys[0], keys[1]) * 0.125).astype(BF)
    vals = [dot(prob_ref[head], grad_ref[...], TN) for head in range(2)]
    dv_ref[...] = jnp.where(wide, vals[0], vals[1]).astype(BF)


def attend_back(qkv, grad, probs):
    seq, cols = qkv.shape
    pairs = cols // (3 * LANES)

    def col(part):
        return pl.BlockSpec((seq, LANES), lambda p: (0, part * pairs + p))

    square = pl.BlockSpec((2, seq, seq), lambda p: (p, 0, 0))
    return pl.pallas_call(
        functools.partial(attend_back_kernel, tile=128),
        grid=(pairs,),
        in_specs=[col(0), col(1), col(2), col(0), square],
        out_specs=[col(0), col(0), col(0), square],
        out_shape=[jax.ShapeDtypeStruct((seq, pairs * LANES), BF)] * 3
        + [jax.ShapeDtypeStruct((2 * pairs, seq, seq), BF)],
        compiler_params=pltpu.CompilerParams(vmem_limit_bytes=40 * MIB),
        name="attend_back",
    )(qkv, qkv, qkv, grad, probs)


def table_kernel(*refs, count):
    *score_refs, bucket_ref, out_ref = refs
    marks = bucket_ref[...]
    tile, seq = marks.shape
    ids = lax.broadcasted_iota(jnp.int32, (tile, count, seq), 1)
    onehot = (jnp.broadcast_to(marks[:, None, :], ids.shape) == ids).astype(F32)
    onehot = onehot.astype(BF).reshape(tile * count, seq)

    @pl.when(pl.program_id(0) == 0)
    def _():
        out_ref[...] = jnp.zeros_like(out_ref)

    at = 0
    for ref in score_refs:
        block = ref[...].reshape(ref.shape[0] * tile, seq)
        out_ref[at : at + block.shape[0], :] += dot(block, onehot, NT)
        at += block.shape[0]


def table_back(scores, buckets, count):
    seq = buckets.shape[0]
    heads = sum(s.shape[0] for s in scores)
    tile = 16
    sums = pl.pallas_call(
        functools.partial(table_kernel, count=count),
        grid=(seq // tile,),
        in_specs=[pl.BlockSpec((s.shape[0], tile, seq), lambda i: (0, i, 0)) for s in scores]
        + [pl.BlockSpec((tile, seq), lambda i: (i, 0))],
        out_specs=pl.BlockSpec((heads * tile, tile * count), lambda i: (0, 0)),
        out_shape=jax.ShapeDtypeStruct((heads * tile, tile * count), F32),
        compiler_params=pltpu.CompilerParams(vmem_limit_bytes=40 * MIB),
        name="table_back",
    )(*scores, buckets)
    sums = sums.reshape(heads, tile, tile, count)
    same = jnp.eye(tile, dtype=F32)[None, :, :, None]
    return jnp.sum(sums * same, axis=(1, 2)).T


def flat(ref):
    block = ref[...]
    return block.astype(F32).reshape(-1, block.shape[-1]).astype(BF)


def expert_kernel(
    base_ref,
    x_ref,
    g_ref,
    other_ref,
    gate_ref,
    up_ref,
    down_ref,
    router_ref,
    out_ref,
    back_ref,
    hidden_ref,
    gate_back_ref,
    up_back_ref,
    route_ref,
):
    expert = pl.program_id(0)
    x = flat(x_ref)
    g = flat(g_ref)
    lanes = lax.broadcasted_iota(jnp.int32, (x.shape[0], LANES), 1)
    sign = (lanes == base_ref[0] + expert).astype(F32) - (lanes == other_ref[0]).astype(F32)
    logits = dot(x, router_ref[...])
    apart = jnp.sum(sign * (logits[:, :LANES] + logits[:, LANES:]), axis=-1, keepdims=True)
    weight = 1.0 / (1.0 + jnp.exp(-apart))
    gate = dot(x, gate_ref[0], NT)
    up = dot(x, up_ref[0], NT)
    grad = dot(g, down_ref[0], NT)
    scale = 0.7978845608028654
    square = gate * gate
    bent = jnp.tanh(scale * gate * (1.0 + 0.044715 * square))
    half = 0.5 + 0.5 * bent
    act = gate * half
    slope = half + 0.5 * gate * (1.0 - bent * bent) * (scale + 3 * 0.044715 * scale * square)
    hidden = act * up
    mark = weight * (1.0 - weight) * jnp.sum(hidden * grad, axis=-1, keepdims=True)
    mark = (mark * sign).astype(BF)
    grad = grad * weight
    up_back = (grad * act).astype(BF)
    gate_back = (grad * up * slope).astype(BF)
    hidden_ref[0] = (hidden * weight).astype(BF)
    gate_back_ref[0] = gate_back
    up_back_ref[0] = up_back
    out = dot(hidden.astype(BF), down_ref[0]) * weight
    out_ref[...] = out.reshape(out_ref.shape).astype(BF)
    back = dot(gate_back, gate_ref[0]) + dot(up_back, up_ref[0])
    back += dot(mark, router_ref[:, :LANES], NT)
    back_ref[...] = back.reshape(back_ref.shape).astype(BF)
    part = dot(mark, x, TN)

    @pl.when(expert == 0)
    def _():
        route_ref[...] = jnp.zeros_like(route_ref)

    route_ref[...] += part


def expert_chunk(base, x, g, other, gate_w, up_w, down_w, router_pair):
    sources, here, slots, width = x.shape
    hidden = down_w.shape[1]
    count = sources * slots
    rows = pl.BlockSpec((sources, 1, slots, width), lambda e: (0, e, 0, 0))
    middle = pl.BlockSpec((1, count, hidden), lambda e: (e, 0, 0))
    weights = pl.BlockSpec((1, hidden, width), lambda e: (e, 0, 0))
    return pl.pallas_call(
        expert_kernel,
        grid=(here,),
        in_specs=[
            pl.BlockSpec(memory_space=pltpu.SMEM),
            rows,
            rows,
            pl.BlockSpec((1, count, 1), lambda e: (e, 0, 0)),
            weights,
            weights,
            weights,
            pl.BlockSpec((width, 2 * LANES), lambda e: (0, 0)),
        ],
        out_specs=[rows, rows, middle, middle, middle, pl.BlockSpec((LANES, width), lambda e: (0, 0))],
        out_shape=[jax.ShapeDtypeStruct(x.shape, BF)] * 2
        + [jax.ShapeDtypeStruct((here, count, hidden), BF)] * 3
        + [jax.ShapeDtypeStruct((LANES, width), F32)],
        compiler_params=pltpu.CompilerParams(vmem_limit_bytes=56 * MIB),
        name="experts",
    )(base, x, g, other, gate_w, up_w, down_w, router_pair)


def weight_kernel(*refs, chunks):
    xs, gs, hidden, gates, ups = (refs[i * chunks : (i + 1) * chunks] for i in range(5))
    gate_ref, up_ref, down_ref = refs[5 * chunks :]
    x = jnp.concatenate([flat(ref) for ref in xs], 0)
    gate_ref[0] = dot(jnp.concatenate([ref[0] for ref in gates], 0), x, TN)
    up_ref[0] = dot(jnp.concatenate([ref[0] for ref in ups], 0), x, TN)
    g = jnp.concatenate([flat(ref) for ref in gs], 0)
    down_ref[0] = dot(jnp.concatenate([ref[0] for ref in hidden], 0), g, TN)


def weight_grads(xs, gs, hidden, gates, ups):
    sources, here, slots, width = xs[0].shape
    depth = hidden[0].shape[2]
    rows = pl.BlockSpec((sources, 1, slots, width), lambda e: (0, e, 0, 0))
    middle = pl.BlockSpec((1, sources * slots, depth), lambda e: (e, 0, 0))
    chunks = len(xs)
    return pl.pallas_call(
        functools.partial(weight_kernel, chunks=chunks),
        grid=(here,),
        in_specs=[rows] * (2 * chunks) + [middle] * (3 * chunks),
        out_specs=[pl.BlockSpec((1, depth, width), lambda e: (e, 0, 0))] * 3,
        out_shape=[jax.ShapeDtypeStruct((here, depth, width), F32)] * 3,
        compiler_params=pltpu.CompilerParams(vmem_limit_bytes=58 * MIB),
        name="expert_weight_grads",
    )(*xs, *gs, *hidden, *gates, *ups)


def body(
    n_expert,
    n_tensor,
    inputs,
    gain_one,
    w_query,
    w_key,
    w_value,
    w_out,
    rel_table,
    gain_two,
    router,
    w_gate,
    w_up,
    w_down,
    routes,
    buckets,
    grad_out,
):
    rows, width = inputs.shape
    experts = router.shape[1]
    here = w_gate.shape[0]
    tokens = routes.shape[0]
    cap = (5 * rows * TOP + 4 * experts - 1) // (4 * experts)
    seq = buckets.shape[0]
    share = seq // rows
    count = rel_table.shape[0]
    head_cols = w_query.shape[1]
    at_expert = lax.axis_index("expert")
    at_tensor = lax.axis_index("tensor")
    both = ("tensor", "expert")

    def swap(value, step):
        return lax.ppermute(value, "tensor", [(i, i ^ step) for i in range(n_tensor)])

    def exchange(value):
        return lax.all_to_all(value, "expert", split_axis=0, concat_axis=0, tiled=True)

    packed = jnp.concatenate([w_query, w_key, w_value, w_out.T], 1)
    strip = width // n_expert
    packed = lax.dynamic_slice_in_dim(packed, at_expert * strip, strip, 0)
    attn_w = lax.all_gather(packed, both, axis=0, tiled=True).reshape(n_tensor, width, 4 * head_cols)
    table_all = lax.all_gather(rel_table.T, "tensor", axis=0, tiled=True)

    labels = jnp.arange(experts, dtype=jnp.int32)
    grouped = routes.T.reshape(TOP, n_expert * n_tensor, rows)
    marks = (grouped[:, :, None, :] == labels[:, None]).astype(BF)
    order = jnp.arange(rows, dtype=jnp.int32)
    earlier = (order[:, None] < order[None, :]).astype(BF)
    ahead = jnp.einsum("kges,st->kget", marks, earlier, preferred_element_type=F32)
    first_count = jnp.sum(marks[0].astype(F32), axis=-1, keepdims=True)
    ahead = ahead + jnp.stack([jnp.zeros_like(first_count), first_count])
    places = jnp.sum(ahead * marks.astype(F32), axis=2).astype(jnp.int32)
    slot_ids = jnp.where(places < cap, grouped * cap + places, -1)
    slot_ids = slot_ids.reshape(TOP, n_expert, n_tensor, rows)
    choices = grouped.reshape(TOP, n_expert, n_tensor, rows)
    local = slot_ids - at_expert * (here * cap)
    slot_here = jnp.arange(here * cap, dtype=jnp.int32)[:, None]
    partner = jnp.sum(
        jnp.where(local[0][:, :, None, :] == slot_here, choices[1][:, :, None, :], 0)
        + jnp.where(local[1][:, :, None, :] == slot_here, choices[0][:, :, None, :], 0),
        axis=-1,
    ).reshape(n_expert, n_tensor, here, cap)
    slot_all = jnp.arange(experts * cap, dtype=jnp.int32)[:, None]
    own_ids = lax.dynamic_index_in_dim(slot_ids, at_expert, 1, keepdims=False)
    tables, partners = [], []
    for step in range(n_tensor):
        ids = lax.dynamic_index_in_dim(own_ids, at_tensor ^ step, 1, keepdims=False)
        tables.append(((ids[0] == slot_all) | (ids[1] == slot_all)).astype(BF))
        pick = lax.dynamic_index_in_dim(partner, at_tensor ^ step, 1, keepdims=False)
        partners.append(jnp.transpose(pick, (1, 0, 2)).reshape(here, n_expert * cap, 1))

    def dispatch(value):
        def buffer(table, part):
            return exchange(dot(table, part).astype(BF).reshape(n_expert, here, cap, width))

        far = [swap(value, step) for step in range(2, n_tensor)]
        own = buffer(tables[0], value)
        return [own, swap(own, 1)] + [
            buffer(tables[step], part) for step, part in zip(range(2, n_tensor), far)
        ]

    def collect(parts):
        total = None
        for step in list(range(n_tensor - 1, 1, -1)):
            back = exchange(parts[step]).reshape(experts * cap, width)
            mixed = swap(dot(tables[step], back, TN).astype(BF), step).astype(F32)
            total = mixed if total is None else total + mixed
        near = (parts[0].astype(F32) + swap(parts[1], 1).astype(F32)).astype(BF)
        near = dot(tables[0], exchange(near).reshape(experts * cap, width), TN)
        return near if total is None else near + total

    def whole_seq(value):
        if share == 1:
            return value
        groups = [[i * share + j for j in range(share)] for i in range(n_tensor // share)]
        return lax.all_gather(value, "tensor", axis=0, tiled=True, axis_index_groups=groups)

    def own_rows(value):
        if share == 1:
            return value
        return lax.dynamic_slice_in_dim(value, (at_tensor % share) * rows, rows, 0)

    grad_slots = dispatch(grad_out)

    inputs_f = inputs.astype(F32)
    normed_one = rms_scale(inputs_f, gain_one).astype(BF)
    attn_in = whole_seq(normed_one)
    pairs = head_cols // LANES
    bias_rows = jnp.pad(table_all, ((0, 0), (0, LANES - count)))
    bias_rows = bias_rows.reshape(n_tensor, pairs, 2, LANES)
    qkv, probs, attended = [], [], []
    resid = inputs_f
    for group in range(n_tensor):
        projected = dot(attn_in, attn_w[group, :, : 3 * head_cols]).astype(BF)
        mixed, weights = attend(projected, buckets, bias_rows[group])
        mixed = own_rows(mixed)
        qkv.append(projected)
        probs.append(weights)
        attended.append(mixed)
        resid = resid + dot(mixed, attn_w[group, :, 3 * head_cols :], NT)

    normed_two = rms_scale(resid, gain_two)
    token_slots = dispatch(normed_two.astype(BF))

    counts = jnp.sum((routes.T[:, None, :] == labels[:, None]).astype(F32), axis=(0, 2))
    route_share = counts / (tokens * TOP)

    def losses(normed, router_w):
        logits = jnp.dot(normed, router_w, precision=highest)
        router_probs = jax.nn.softmax(logits, axis=-1)
        log_totals = jax.nn.logsumexp(logits, axis=-1)
        balance = experts * jnp.sum(route_share * jnp.sum(router_probs, axis=0)) / tokens
        return balance, jnp.sum(log_totals * log_totals) / tokens

    (balance_part, zloss_part), losses_back = jax.vjp(losses, normed_two, router)
    normed_grad, router_grad = losses_back(
        (jnp.asarray(balance_weight, F32), jnp.asarray(zloss_weight, F32))
    )

    router_high = router.astype(BF)
    router_low = (router - router_high.astype(F32)).astype(BF)
    fill = ((0, 0), (0, LANES - experts))
    router_pair = jnp.concatenate([jnp.pad(router_high, fill), jnp.pad(router_low, fill)], 1)
    base = jnp.full((1,), at_expert * here, jnp.int32)
    gate_w = jnp.swapaxes(w_gate, 1, 2)
    up_w = jnp.swapaxes(w_up, 1, 2)

    def rows_in(value):
        if cap % 8 == 0:
            return value
        return jnp.swapaxes(value, 0, 1).reshape(1, here, n_expert * cap, width)

    def rows_out(value):
        if cap % 8 == 0:
            return value
        return jnp.swapaxes(value.reshape(here, n_expert, cap, width), 0, 1)

    token_slots = [rows_in(v) for v in token_slots]
    grad_slots = [rows_in(v) for v in grad_slots]
    done = [
        expert_chunk(base, x, g, other, gate_w, up_w, w_down, router_pair)
        for x, g, other in zip(token_slots, grad_slots, partners)
    ]
    moe_grad = collect([rows_out(d[1]) for d in done])
    mixture = collect([rows_out(d[0]) for d in done])
    router_grad = router_grad + sum(d[5] for d in done)[:experts].T
    gate_grad, up_grad, down_grad = weight_grads(
        token_slots, grad_slots, [d[2] for d in done], [d[3] for d in done], [d[4] for d in done]
    )

    grad_f = grad_out.astype(F32)
    resid_norm_grad, gain_two_grad = jax.vjp(rms_scale, resid, gain_two)[1](normed_grad + moe_grad)
    resid_grad = grad_f + resid_norm_grad
    attn_grad = resid_grad.astype(BF)
    attn_grad_seq = whole_seq(attn_grad)

    normed_one_grad = jnp.zeros((rows, width), F32)
    scattered, score_grads = [], []
    for group in range(n_tensor):
        out_w = attn_w[group, :, 3 * head_cols :]
        mixed_grad = dot(attn_grad_seq, out_w).astype(BF)
        *parts, score = attend_back(qkv[group], mixed_grad, probs[group])
        score_grads.append(score)
        back = own_rows(jnp.concatenate(parts, 1))
        normed_one_grad = normed_one_grad + dot(back, attn_w[group, :, : 3 * head_cols], NT)
        weight_part = jnp.concatenate(
            [dot(normed_one, back, TN).astype(BF), dot(attn_grad, attended[group], TN).astype(BF)], 1
        )
        scattered.append(lax.psum_scatter(weight_part, "expert", scatter_dimension=0, tiled=True))
    summed = lax.psum_scatter(jnp.stack(scattered), "tensor", scatter_dimension=0, tiled=False)
    attn_w_grad = lax.all_gather(summed, "expert", axis=0, tiled=True).astype(F32)

    input_norm_grad, gain_one_grad = jax.vjp(rms_scale, inputs_f, gain_one)[1](normed_one_grad)
    input_grad = resid_grad + input_norm_grad
    table_grad = table_back(score_grads, buckets, count) / share
    output = (resid + mixture).astype(BF)

    small = lax.psum(
        (router_grad, gain_one_grad, gain_two_grad, jnp.stack([balance_part, zloss_part]), table_grad),
        ("expert", "tensor"),
    )
    router_total, gain_one_total, gain_two_total, loss_total, table_total = small
    table_own = lax.dynamic_slice_in_dim(
        table_total, at_tensor * rel_table.shape[1], rel_table.shape[1], 1
    )
    return (
        output,
        input_grad,
        gain_one_total,
        attn_w_grad[:, :head_cols],
        attn_w_grad[:, head_cols : 2 * head_cols],
        attn_w_grad[:, 2 * head_cols : 3 * head_cols],
        attn_w_grad[:, 3 * head_cols :].T,
        table_own,
        gain_two_total,
        router_total,
        jnp.swapaxes(gate_grad, 1, 2),
        jnp.swapaxes(up_grad, 1, 2),
        down_grad,
        loss_total,
    )


def solution(mesh):
    return jax.shard_map(
        functools.partial(body, mesh.shape["expert"], mesh.shape["tensor"]),
        mesh=mesh,
        in_specs=(
            P(("expert", "tensor"), None),
            P(),
            P(None, "tensor"),
            P(None, "tensor"),
            P(None, "tensor"),
            P("tensor", None),
            P(None, "tensor"),
            P(),
            P(),
            P("expert", None, "tensor"),
            P("expert", None, "tensor"),
            P("expert", "tensor", None),
            P(),
            P(),
            P(("expert", "tensor"), None),
        ),
        out_specs=(
            P(("expert", "tensor"), None),
            P(("expert", "tensor"), None),
            P(),
            P(None, "tensor"),
            P(None, "tensor"),
            P(None, "tensor"),
            P("tensor", None),
            P(None, "tensor"),
            P(),
            P(),
            P("expert", None, "tensor"),
            P("expert", None, "tensor"),
            P("expert", "tensor", None),
            P(),
        ),
        check_vma=False,
    )
```

```python
import functools

import jax
import jax.numpy as jnp
from jax import lax
from jax.experimental import pallas as pl
from jax.experimental.pallas import tpu as pltpu
from jax.sharding import PartitionSpec as P

HEAD_DIM = 64
TOP = 2
LANES = 128
MIB = 2**20

epsilon = 1e-06
balance_weight = 0.01
zloss_weight = 0.001
highest = lax.Precision.HIGHEST

BF = jnp.bfloat16
F32 = jnp.float32
NN = (((1,), (0,)), ((), ()))
NT = (((1,), (1,)), ((), ()))
TN = (((0,), (0,)), ((), ()))


def dot(left, right, dims=NN):
    return lax.dot_general(left, right, dims, preferred_element_type=F32)


def rms_scale(rows_in, gain):
    inverse = lax.rsqrt(jnp.mean(rows_in * rows_in, axis=-1, keepdims=True) + epsilon)
    return rows_in * inverse * gain


def drop(kernel, at, count):
    def run(*refs):
        kernel(*refs[:at], *refs[at + count :])

    return run


def launch(kernel, operands, after, *, grid, in_specs, out_specs, out_shape, name, flops, scratch=(), moved=0):
    held = [value for value in after if value is not None]
    sizes = [jax.ShapeDtypeStruct(v.shape, v.dtype) for v in operands] + jax.tree.leaves(out_shape)
    moved = moved or sum(v.size * v.dtype.itemsize for v in sizes)
    return pl.pallas_call(
        drop(kernel, len(operands), len(held)),
        grid=grid,
        in_specs=list(in_specs) + [pl.BlockSpec(memory_space=pl.ANY)] * len(held),
        out_specs=out_specs,
        out_shape=out_shape,
        scratch_shapes=scratch,
        compiler_params=pltpu.CompilerParams(vmem_limit_bytes=58 * MIB),
        cost_estimate=pl.CostEstimate(flops=flops, bytes_accessed=moved, transcendentals=0),
        name=name,
    )(*operands, *held)


def lookup(row, index):
    table = jnp.broadcast_to(row, (index.shape[0], LANES))
    parts = [
        jnp.take_along_axis(table, index[:, at : at + LANES], axis=1)
        for at in range(0, index.shape[1], LANES)
    ]
    return jnp.concatenate(parts, axis=1)


def attend_kernel(x_ref, w_ref, bucket_ref, table_ref, qkv_ref, mixed_ref, prob_ref, out_ref):
    seq = x_ref.shape[0]
    tile = 128
    low = lax.broadcasted_iota(jnp.int32, (tile, LANES), 1) < HEAD_DIM
    for part in range(3):
        qkv_ref[part] = dot(x_ref[...], w_ref[part, 0, 0], NT).astype(BF)
    for start in range(0, seq, tile):
        rows = pl.ds(start, tile)
        query = qkv_ref[0, rows, :]
        mixed = []
        for head in range(2):
            part = jnp.where(low if head == 0 else ~low, query, jnp.zeros_like(query))
            scores = dot(part, qkv_ref[1], NT) * 0.125 + lookup(
                table_ref[0, head : head + 1, :], bucket_ref[rows, :]
            )
            scores = jnp.exp(scores - jnp.max(scores, axis=-1, keepdims=True))
            weights = (scores / jnp.sum(scores, axis=-1, keepdims=True)).astype(BF)
            prob_ref[head, rows, :] = weights
            mixed.append(dot(weights, qkv_ref[2]))
        mixed_ref[rows, :] = jnp.where(low, mixed[0], mixed[1]).astype(BF)
    out = dot(mixed_ref[...], w_ref[3, 0, 0])

    @pl.when(pl.program_id(0) == 0)
    def _():
        out_ref[...] = out

    @pl.when(pl.program_id(0) > 0)
    def _():
        out_ref[...] += out


def attend(x, weights, buckets, table, after):
    seq, width = x.shape
    _, pairs, groups, _, _ = weights.shape
    steps = pairs * groups
    full = pl.BlockSpec((seq, width), lambda i: (0, 0))
    col = pl.BlockSpec((seq, LANES), lambda i: (0, i))
    return launch(
        attend_kernel,
        (x, weights, buckets, table),
        after,
        grid=(steps,),
        in_specs=[
            full,
            pl.BlockSpec((4, 1, 1, LANES, width), lambda i: (0, i % pairs, i // pairs, 0, 0)),
            pl.BlockSpec((seq, seq), lambda i: (0, 0)),
            pl.BlockSpec((1, 2, LANES), lambda i: (i, 0, 0)),
        ],
        out_specs=[
            pl.BlockSpec((3, seq, LANES), lambda i: (0, 0, i)),
            col,
            pl.BlockSpec((2, seq, seq), lambda i: (i, 0, 0)),
            full,
        ],
        out_shape=[
            jax.ShapeDtypeStruct((3, seq, steps * LANES), BF),
            jax.ShapeDtypeStruct((seq, steps * LANES), BF),
            jax.ShapeDtypeStruct((2 * steps, seq, seq), BF),
            jax.ShapeDtypeStruct((seq, width), F32),
        ],
        name="attend",
        flops=steps * seq * LANES * 2 * (4 * width + 4 * seq),
    )


def attend_back_kernel(
    x_ref, grad_ref, w_ref, qkv_ref, mixed_ref, prob_ref, weight_ref, score_ref, normed_ref, part_ref
):
    seq = x_ref.shape[0]
    tile = 128
    low = lax.broadcasted_iota(jnp.int32, (tile, LANES), 1) < HEAD_DIM
    mixed_grad = dot(grad_ref[...], w_ref[3, 0, 0], NT).astype(BF)
    part_ref[...] = mixed_grad
    queries = []
    for start in range(0, seq, tile):
        rows = pl.ds(start, tile)
        grad = part_ref[rows, :]
        back = []
        for head in range(2):
            part = jnp.where(low if head == 0 else ~low, grad, jnp.zeros_like(grad))
            weights = prob_ref[head, rows, :].astype(F32)
            weight_grad = dot(part, qkv_ref[2], NT)
            score = weights * (
                weight_grad - jnp.sum(weights * weight_grad, axis=-1, keepdims=True)
            )
            score = score.astype(BF)
            score_ref[head, rows, :] = score
            back.append(dot(score, qkv_ref[1]))
        queries.append((jnp.where(low, back[0], back[1]) * 0.125).astype(BF))
    wide = lax.broadcasted_iota(jnp.int32, (seq, LANES), 1) < HEAD_DIM
    keys = [dot(score_ref[head], qkv_ref[0], TN) for head in range(2)]
    vals = [dot(prob_ref[head], mixed_grad, TN) for head in range(2)]
    back = jnp.concatenate(
        [
            jnp.concatenate(queries, 0),
            (jnp.where(wide, keys[0], keys[1]) * 0.125).astype(BF),
            jnp.where(wide, vals[0], vals[1]).astype(BF),
        ],
        1,
    )
    weight_ref[:3, 0, 0] = dot(back, x_ref[...], TN).reshape(3, LANES, -1).astype(BF)
    weight_ref[3, 0, 0] = dot(mixed_ref[...], grad_ref[...], TN).astype(BF)
    normed = dot(back, w_ref[:3, 0, 0].reshape(3 * LANES, -1))

    @pl.when(pl.program_id(0) == 0)
    def _():
        normed_ref[...] = normed

    @pl.when(pl.program_id(0) > 0)
    def _():
        normed_ref[...] += normed


def attend_back(x, grad, weights, qkv, mixed, probs, after):
    seq, width = x.shape
    _, pairs, groups, _, _ = weights.shape
    steps = pairs * groups
    full = pl.BlockSpec((seq, width), lambda i: (0, 0))
    col = pl.BlockSpec((seq, LANES), lambda i: (0, i))
    strip = pl.BlockSpec((4, 1, 1, LANES, width), lambda i: (0, i % pairs, i // pairs, 0, 0))
    square = pl.BlockSpec((2, seq, seq), lambda i: (i, 0, 0))
    return launch(
        attend_back_kernel,
        (x, grad, weights, qkv, mixed, probs),
        after,
        grid=(steps,),
        in_specs=[full, full, strip, pl.BlockSpec((3, seq, LANES), lambda i: (0, 0, i)), col, square],
        out_specs=[strip, square, full],
        out_shape=[
            jax.ShapeDtypeStruct((4, pairs, groups, LANES, width), BF),
            jax.ShapeDtypeStruct(probs.shape, BF),
            jax.ShapeDtypeStruct((seq, width), F32),
        ],
        scratch=[pltpu.VMEM((seq, LANES), BF)],
        name="attend_back",
        flops=steps * seq * LANES * 2 * (8 * width + 8 * seq),
    )


def table_kernel(*refs):
    *score_refs, bucket_ref, out_ref = refs
    marks = bucket_ref[...]
    tile, seq = marks.shape
    count = out_ref.shape[1] // tile
    ids = lax.broadcasted_iota(jnp.int32, (tile, count, seq), 1)
    onehot = (jnp.broadcast_to(marks[:, None, :], ids.shape) == ids).astype(F32)
    onehot = onehot.astype(BF).reshape(tile * count, seq)
    block = jnp.concatenate([ref[...].reshape(-1, seq) for ref in score_refs], 0)
    sums = dot(block, onehot, NT)

    @pl.when(pl.program_id(0) == 0)
    def _():
        out_ref[...] = sums

    @pl.when(pl.program_id(0) > 0)
    def _():
        out_ref[...] += sums


def table_back(scores, buckets, count, after):
    heads = sum(part.shape[0] for part in scores)
    seq = buckets.shape[0]
    tile = 16
    sums = launch(
        table_kernel,
        (*scores, buckets),
        after,
        grid=(seq // tile,),
        in_specs=[pl.BlockSpec((part.shape[0], tile, seq), lambda i: (0, i, 0)) for part in scores]
        + [pl.BlockSpec((tile, seq), lambda i: (i, 0))],
        out_specs=pl.BlockSpec((heads * tile, tile * count), lambda i: (0, 0)),
        out_shape=jax.ShapeDtypeStruct((heads * tile, tile * count), F32),
        name="table_back",
        flops=heads * tile * seq * seq * count * 2 * 4,
    )
    sums = sums.reshape(heads, tile, tile, count)
    same = jnp.eye(tile, dtype=F32)[None, :, :, None]
    return jnp.sum(sums * same, axis=(1, 2)).T


def assemble(place, halves, after):
    sources, groups, strip, _ = halves[0].shape
    width = sum(half.shape[3] for half in halves)
    held = [value for value in after if value is not None]

    def kernel(place_ref, *refs):
        refs[-1][0] = jnp.concatenate([ref[0] for ref in refs[: len(halves)]], -1)

    return pl.pallas_call(
        kernel,
        grid_spec=pltpu.PrefetchScalarGridSpec(
            num_scalar_prefetch=1,
            grid=(sources,),
            in_specs=[
                pl.BlockSpec((1, groups, strip, half.shape[3]), lambda i, at, side=side: (at[side, i], 0, 0, 0))
                for side, half in enumerate(halves)
            ]
            + [pl.BlockSpec(memory_space=pl.ANY)] * len(held),
            out_specs=pl.BlockSpec((1, groups, strip, width), lambda i, at: (i, 0, 0, 0)),
        ),
        out_shape=jax.ShapeDtypeStruct((sources, groups, strip, width), BF),
        cost_estimate=pl.CostEstimate(flops=0, bytes_accessed=4 * sources * groups * strip * width, transcendentals=0),
        name="assemble",
    )(place, *halves, *held)


def copy_kernel(from_ref, to_ref):
    to_ref[...] = from_ref[...]


def hold(value, after):
    full = pl.BlockSpec(value.shape, lambda i: (0,) * value.ndim)
    return launch(
        copy_kernel,
        (value,),
        after,
        grid=(1,),
        in_specs=[full],
        out_specs=full,
        out_shape=jax.ShapeDtypeStruct(value.shape, value.dtype),
        name="hold",
        flops=0,
    )


def stack(place, parts, after):
    shape = parts[0].shape
    held = [value for value in after if value is not None]
    count = len(parts)

    def kernel(place_ref, *refs):
        for i in range(count):

            @pl.when(pl.program_id(0) == i)
            def _():
                refs[-1][...] = refs[i][...]

    full = pl.BlockSpec(shape, lambda s, at: (0,) * len(shape))
    return pl.pallas_call(
        kernel,
        grid_spec=pltpu.PrefetchScalarGridSpec(
            num_scalar_prefetch=1,
            grid=(count,),
            in_specs=[full] * count + [pl.BlockSpec(memory_space=pl.ANY)] * len(held),
            out_specs=pl.BlockSpec(shape, lambda s, at: (at[s],) + (0,) * (len(shape) - 1)),
        ),
        out_shape=jax.ShapeDtypeStruct((count * shape[0],) + shape[1:], BF),
        compiler_params=pltpu.CompilerParams(vmem_limit_bytes=58 * MIB),
        name="stack",
    )(place, *parts, *held)


def sum_kernel(*refs):
    *parts, out_ref = refs
    total = parts[0][...].astype(F32)
    for ref in parts[1:]:
        total += ref[...].astype(F32)
    out_ref[...] = total.astype(out_ref.dtype)


def add(*operands):
    *parts, after = operands
    shape = parts[0].shape
    if parts[0].ndim > 2:
        block = pl.BlockSpec((1,) + shape[1:], lambda i: (i,) + (0,) * (len(shape) - 1))
    else:
        block = pl.BlockSpec(shape, lambda i: (0, 0))
    return launch(
        sum_kernel,
        parts,
        after,
        grid=(shape[0] if len(shape) > 2 else 1,),
        in_specs=[block] * len(parts),
        out_specs=block,
        out_shape=jax.ShapeDtypeStruct(shape, parts[0].dtype),
        name="add",
        flops=parts[0].size,
    )


def dispatch_kernel(id_ref, x_ref, out_ref):
    count = out_ref.shape[0]
    slot = lax.broadcasted_iota(jnp.int32, (count, x_ref.shape[0]), 0) + pl.program_id(0) * count
    onehot = (slot == id_ref[0:1, :]) | (slot == id_ref[1:2, :])
    out_ref[...] = dot(onehot.astype(F32).astype(BF), x_ref[...]).astype(BF)


def to_slots(ids, value, slots, after):
    rows, width = value.shape
    steps = 4
    return launch(
        dispatch_kernel,
        (ids, value),
        after,
        grid=(steps,),
        in_specs=[
            pl.BlockSpec((TOP, rows), lambda i: (0, 0)),
            pl.BlockSpec((rows, width), lambda i: (0, 0)),
        ],
        out_specs=pl.BlockSpec((slots // steps, width), lambda i: (i, 0)),
        out_shape=jax.ShapeDtypeStruct((slots, width), BF),
        name="to_slots",
        flops=slots * rows * width * 2,
    )


def collect_kernel(id_ref, slot_ref, *refs):
    *more, out_ref = refs
    rows = out_ref.shape[0]
    slot = lax.broadcasted_iota(jnp.int32, (rows, slot_ref.shape[0]), 1)
    onehot = (slot == id_ref[:, 0:1]) | (slot == id_ref[:, 1:2])
    total = dot(onehot.astype(F32).astype(BF), slot_ref[...])
    for ref in more:
        total += ref[...].astype(F32)
    out_ref[...] = total.astype(out_ref.dtype)


def to_tokens(ids, slots, more, kind, after):
    rows = ids.shape[0]
    count, width = slots.shape
    steps = 2
    block = pl.BlockSpec((rows // steps, width), lambda i: (i, 0))
    return launch(
        collect_kernel,
        (ids, slots, *more),
        after,
        grid=(steps,),
        in_specs=[
            pl.BlockSpec((rows // steps, TOP), lambda i: (i, 0)),
            pl.BlockSpec((count, width), lambda i: (0, 0)),
        ]
        + [block] * len(more),
        out_specs=block,
        out_shape=jax.ShapeDtypeStruct((rows, width), kind),
        name="to_tokens",
        flops=count * rows * width * 2,
    )


def flat(ref):
    block = ref[...]
    return block.astype(F32).reshape(-1, block.shape[-1]).astype(BF)


def expert_kernel(
    base_ref,
    x_ref,
    g_ref,
    other_ref,
    gate_ref,
    up_ref,
    down_ref,
    router_ref,
    out_ref,
    back_ref,
    hidden_ref,
    gate_back_ref,
    up_back_ref,
    route_ref,
):
    expert = pl.program_id(0)
    x = flat(x_ref)
    g = flat(g_ref)
    lanes = lax.broadcasted_iota(jnp.int32, (x.shape[0], LANES), 1)
    sign = (lanes == base_ref[0] + expert).astype(F32) - (lanes == other_ref[0]).astype(F32)
    logits = dot(x, router_ref[...])
    apart = jnp.sum(sign * (logits[:, :LANES] + logits[:, LANES:]), axis=-1, keepdims=True)
    weight = 1.0 / (1.0 + jnp.exp(-apart))
    gate = dot(x, gate_ref[0], NT)
    up = dot(x, up_ref[0], NT)
    grad = dot(g, down_ref[0], NT)
    scale = 0.7978845608028654
    square = gate * gate
    bent = jnp.tanh(scale * gate * (1.0 + 0.044715 * square))
    half = 0.5 + 0.5 * bent
    act = gate * half
    slope = half + 0.5 * gate * (1.0 - bent * bent) * (scale + 3 * 0.044715 * scale * square)
    hidden = act * up
    mark = weight * (1.0 - weight) * jnp.sum(hidden * grad, axis=-1, keepdims=True)
    mark = (mark * sign).astype(BF)
    grad = grad * weight
    up_back = (grad * act).astype(BF)
    gate_back = (grad * up * slope).astype(BF)
    hidden_ref[0] = (hidden * weight).astype(BF)
    gate_back_ref[0] = gate_back
    up_back_ref[0] = up_back
    out = dot(hidden.astype(BF), down_ref[0]) * weight
    out_ref[...] = out.reshape(out_ref.shape).astype(BF)
    back = dot(gate_back, gate_ref[0]) + dot(up_back, up_ref[0])
    back += dot(mark, router_ref[:, :LANES], NT)
    back_ref[...] = back.reshape(back_ref.shape).astype(BF)
    part = dot(mark, x, TN)

    @pl.when(expert == 0)
    def _():
        route_ref[...] = jnp.zeros_like(route_ref)

    route_ref[...] += part


def expert_chunk(base, x, g, other, gate_w, up_w, down_w, router_pair, after):
    sources, here, slots, width = x.shape
    hidden = down_w.shape[1]
    count = sources * slots
    rows = pl.BlockSpec((sources, 1, slots, width), lambda e: (0, e, 0, 0))
    middle = pl.BlockSpec((1, count, hidden), lambda e: (e, 0, 0))
    weights = pl.BlockSpec((1, hidden, width), lambda e: (e, 0, 0))
    return launch(
        expert_kernel,
        (base, x, g, other, gate_w, up_w, down_w, router_pair),
        after,
        grid=(here,),
        in_specs=[
            pl.BlockSpec(memory_space=pltpu.SMEM),
            rows,
            rows,
            pl.BlockSpec((1, count, 1), lambda e: (e, 0, 0)),
            weights,
            weights,
            weights,
            pl.BlockSpec((width, 2 * LANES), lambda e: (0, 0)),
        ],
        out_specs=[rows, rows, middle, middle, middle, pl.BlockSpec((LANES, width), lambda e: (0, 0))],
        out_shape=[jax.ShapeDtypeStruct(x.shape, BF)] * 2
        + [jax.ShapeDtypeStruct((here, count, hidden), BF)] * 3
        + [jax.ShapeDtypeStruct((LANES, width), F32)],
        name="experts",
        flops=12 * here * count * width * hidden * 2,
    )


def weight_kernel(*refs, chunks):
    xs, gs, hidden, gates, ups = (refs[i * chunks : (i + 1) * chunks] for i in range(5))
    gate_ref, up_ref, down_ref = refs[5 * chunks :]
    x = jnp.concatenate([flat(ref) for ref in xs], 0)
    gate_ref[0] = dot(jnp.concatenate([ref[0] for ref in gates], 0), x, TN)
    up_ref[0] = dot(jnp.concatenate([ref[0] for ref in ups], 0), x, TN)
    g = jnp.concatenate([flat(ref) for ref in gs], 0)
    down_ref[0] = dot(jnp.concatenate([ref[0] for ref in hidden], 0), g, TN)


def weight_grads(xs, gs, hidden, gates, ups, after):
    sources, here, slots, width = xs[0].shape
    depth = hidden[0].shape[2]
    rows = pl.BlockSpec((sources, 1, slots, width), lambda e: (0, e, 0, 0))
    middle = pl.BlockSpec((1, sources * slots, depth), lambda e: (e, 0, 0))
    chunks = len(xs)
    return launch(
        functools.partial(weight_kernel, chunks=chunks),
        (*xs, *gs, *hidden, *gates, *ups),
        after,
        grid=(here,),
        in_specs=[rows] * (2 * chunks) + [middle] * (3 * chunks),
        out_specs=[pl.BlockSpec((1, depth, width), lambda e: (e, 0, 0))] * 3,
        out_shape=[jax.ShapeDtypeStruct((here, depth, width), F32)] * 3,
        name="expert_weight_grads",
        flops=4 * here * chunks * sources * slots * width * depth * 2,
    )


def body(
    n_expert,
    n_tensor,
    inputs,
    gain_one,
    w_query,
    w_key,
    w_value,
    w_out,
    rel_table,
    gain_two,
    router,
    w_gate,
    w_up,
    w_down,
    routes,
    buckets,
    grad_out,
):
    rows, width = inputs.shape
    experts = router.shape[1]
    here = w_gate.shape[0]
    tokens = routes.shape[0]
    cap = (5 * rows * TOP + 4 * experts - 1) // (4 * experts)
    slots = experts * cap
    seq = buckets.shape[0]
    share = seq // rows
    count = rel_table.shape[0]
    head_cols = w_query.shape[1]
    at_expert = lax.axis_index("expert")
    at_tensor = lax.axis_index("tensor")
    steps = range(n_tensor)
    far = range(2, n_tensor)
    last = [None]

    def swap(value, step):
        return lax.ppermute(value, "tensor", [(i, i ^ step) for i in range(n_tensor)])

    def exchange(value):
        return lax.all_to_all(value, "expert", split_axis=0, concat_axis=0, tiled=True)

    def ordered(run, *operands, after=()):
        before = last[0] if isinstance(last[0], tuple) else (last[0],)
        result = run(*operands, (*before, *after))
        last[0] = result[0] if isinstance(result, (list, tuple)) else result
        return result

    labels = jnp.arange(experts, dtype=jnp.int32)
    grouped = routes.T.reshape(TOP, n_expert * n_tensor, rows)
    marks = (grouped[:, :, None, :] == labels[:, None]).astype(BF)
    order = jnp.arange(rows, dtype=jnp.int32)
    earlier = (order[:, None] < order[None, :]).astype(BF)
    ahead = jnp.einsum("kges,st->kget", marks, earlier, preferred_element_type=F32)
    first_count = jnp.sum(marks[0].astype(F32), axis=-1, keepdims=True)
    ahead = ahead + jnp.stack([jnp.zeros_like(first_count), first_count])
    places = jnp.sum(ahead * marks.astype(F32), axis=2).astype(jnp.int32)
    slot_ids = jnp.where(places < cap, grouped * cap + places, -1)
    slot_ids = slot_ids.reshape(TOP, n_expert, n_tensor, rows)
    choices = grouped.reshape(TOP, n_expert, n_tensor, rows)

    def relative(value, axis):
        return jnp.stack([lax.dynamic_index_in_dim(value, at_tensor ^ i, axis, keepdims=False) for i in steps])

    own_ids = relative(lax.dynamic_index_in_dim(slot_ids, at_expert, 1, keepdims=False), 1)
    id_rows = [own_ids[i] for i in steps]
    id_cols = jnp.swapaxes(own_ids, 1, 2)
    local = slot_ids - at_expert * (here * cap)
    slot_here = jnp.arange(here * cap, dtype=jnp.int32)[:, None]
    partner = jnp.sum(
        jnp.where(local[0][:, :, None, :] == slot_here, choices[1][:, :, None, :], 0)
        + jnp.where(local[1][:, :, None, :] == slot_here, choices[0][:, :, None, :], 0),
        axis=-1,
    ).reshape(n_expert, n_tensor, here, cap)
    partners = jnp.swapaxes(relative(partner, 1), 1, 2).reshape(n_tensor, here, n_expert * cap, 1)

    def send(step, value, after=()):
        buffer = ordered(to_slots, id_rows[step], value, slots, after=after)
        return exchange(buffer.reshape(n_expert, here, cap, width))

    def home(step, value, more=(), kind=BF, after=()):
        return ordered(to_tokens, id_cols[step], value.reshape(slots, width), more, kind, after=after)

    def gather(value):
        whole = lax.all_gather(value, "tensor", axis=0, tiled=True).reshape(n_tensor, rows, width)
        return [lax.dynamic_index_in_dim(whole, at_tensor ^ i, 0, keepdims=False) for i in steps]

    def everywhere(values):
        total = jnp.concatenate([value.reshape(-1) for value in values])
        for axis, size in (("expert", n_expert), ("tensor", n_tensor)):
            for bit in range(size.bit_length() - 1):
                total = total + lax.ppermute(total, axis, [(i, i ^ (1 << bit)) for i in range(size)])
        totals = []
        for value in values:
            totals.append(total[: value.size].reshape(value.shape))
            total = total[value.size :]
        return totals

    def whole_seq(value):
        if share == 1:
            return value
        groups = [[i * share + j for j in range(share)] for i in range(n_tensor // share)]
        return lax.all_gather(value, "tensor", axis=0, tiled=True, axis_index_groups=groups)

    def own_rows(value):
        if share == 1:
            return value
        return lax.dynamic_slice_in_dim(value, (at_tensor % share) * rows, rows, 0)

    packed = jnp.concatenate([w_query.T, w_key.T, w_value.T, w_out], 0)
    strip = 4 * head_cols // n_expert
    blocks = 4 * head_cols // LANES
    pairs = blocks // 4
    own_w = packed.reshape(4, pairs, 1, LANES, width)
    packed = ordered(hold, lax.dynamic_slice_in_dim(packed, at_expert * strip, strip, 0))
    strips = jnp.stack([swap(packed, i) for i in steps[1:]])
    table_own = jnp.pad(rel_table.T, ((0, 0), (0, LANES - count)))
    table_all = jnp.stack([table_own] + [swap(table_own, i) for i in steps[1:]])
    table_all = table_all.reshape(n_tensor * pairs, 2, LANES)

    inputs_f = inputs.astype(F32)
    normed_one = rms_scale(inputs_f, gain_one).astype(BF)
    attn_in = whole_seq(normed_one)
    grad_far = gather(ordered(hold, grad_out, after=(strips, table_all)))
    own_part = ordered(attend, attn_in, own_w, buckets, table_all[:pairs])

    bits = [1 << i for i in range(1, n_expert.bit_length() - 1)]
    sources = jnp.arange(n_expert, dtype=jnp.int32) ^ at_expert
    halves, places, came = [], [], []
    for half in range(2):
        held, order = strips[None, :, :, half * width // 2 : (half + 1) * width // 2], [0]
        for bit in (bits if half == 0 else bits[::-1]) + [1]:
            came.append(held)
            held = jnp.concatenate([held, lax.ppermute(held, "expert", [(i, i ^ bit) for i in range(n_expert)])], 0)
            order = order + [i ^ bit for i in order]
        halves.append(held)
        where = jnp.asarray([order.index(i) for i in range(n_expert)], jnp.int32)
        places.append(jnp.sum(jnp.where(sources[:, None] == jnp.arange(n_expert), where, 0), 1))
    places = jnp.stack(places).astype(jnp.int32)

    grad_slots = {0: send(0, grad_out, (came[len(bits)], came[-1]))}
    attn_w = ordered(assemble, places, halves)
    attn_w = attn_w.reshape(blocks, n_expert // blocks, n_tensor - 1, strip, width)
    attn_w = jnp.swapaxes(attn_w, 1, 2).reshape(4, pairs, n_tensor - 1, LANES, width)
    rest_part = ordered(attend, attn_in, attn_w, buckets, table_all[pairs:])
    grad_slots[1] = send(1, grad_far[1])
    resid = inputs_f + own_rows(own_part[3] + rest_part[3])
    normed_two = rms_scale(resid, gain_two)
    normed_low = normed_two.astype(BF)

    token_far = gather(normed_low)
    token_slots = {0: send(0, normed_low)}
    for i in far:
        grad_slots[i] = send(i, grad_far[i])

    counts = jnp.sum((routes.T[:, None, :] == labels[:, None]).astype(F32), axis=(0, 2))
    route_share = counts / (tokens * TOP)

    def losses(normed, router_w):
        logits = jnp.dot(normed, router_w, precision=highest)
        router_probs = jax.nn.softmax(logits, axis=-1)
        log_totals = jax.nn.logsumexp(logits, axis=-1)
        balance = experts * jnp.sum(route_share * jnp.sum(router_probs, axis=0)) / tokens
        return balance, jnp.sum(log_totals * log_totals) / tokens

    (balance_part, zloss_part), losses_back = jax.vjp(losses, normed_two, router)
    normed_grad, router_grad = losses_back(
        (jnp.asarray(balance_weight, F32), jnp.asarray(zloss_weight, F32))
    )

    router_high = router.astype(BF)
    router_low = (router - router_high.astype(F32)).astype(BF)
    fill = ((0, 0), (0, LANES - experts))
    router_pair = jnp.concatenate([jnp.pad(router_high, fill), jnp.pad(router_low, fill)], 1)
    base = jnp.full((1,), at_expert * here, jnp.int32)
    gate_w = jnp.swapaxes(w_gate, 1, 2)
    up_w = jnp.swapaxes(w_up, 1, 2)

    def rows_in(value):
        if cap % 8 == 0:
            return value
        return jnp.swapaxes(value, 0, 1).reshape(1, here, n_expert * cap, width)

    def rows_out(value):
        if cap % 8 == 0:
            return value
        return jnp.swapaxes(value.reshape(here, n_expert, cap, width), 0, 1)

    xs, gs, done = {}, {}, {}

    def work(step):
        xs[step], gs[step] = rows_in(token_slots[step]), rows_in(grad_slots[step])
        done[step] = ordered(
            expert_chunk, base, xs[step], gs[step], partners[step], gate_w, up_w, w_down, router_pair
        )

    work(0)
    for i in steps[1:]:
        token_slots[i] = send(i, token_far[i], (*grad_slots.values(),))
    for i in steps[1:]:
        work(i)
    backs = {i: rows_out(done[i][1]) for i in steps}
    outs = {i: rows_out(done[i][0]) for i in steps}
    moe_far, near = [], None
    for i in far:
        moe_far.append(swap(home(i, exchange(backs[i]), after=moe_far[-1:]), i))
        if i == far[0]:
            near = exchange(ordered(add, backs[0], swap(backs[1], 1)))
    gate_grad, up_grad, down_grad = ordered(
        weight_grads,
        *[[v[i] for i in steps] for v in (xs, gs)],
        *[[done[i][j] for i in steps] for j in (2, 3, 4)],
    )
    moe_grad = home(0, near, moe_far, F32)
    router_grad = router_grad + sum(done[i][5] for i in steps)[:experts].T

    grad_f = grad_out.astype(F32)
    resid_norm_grad, gain_two_grad = jax.vjp(rms_scale, resid, gain_two)[1](normed_grad + moe_grad)
    resid_grad = grad_f + resid_norm_grad
    attn_grad = whole_seq(resid_grad.astype(BF))
    out_all = ordered(stack, jnp.arange(n_tensor, dtype=jnp.int32) ^ at_tensor, [outs[i] for i in steps])
    rest_back = ordered(attend_back, attn_in, attn_grad, attn_w, *rest_part[:3])
    own_back = ordered(attend_back, attn_in, attn_grad, own_w, *own_part[:3])
    out_sum = lax.psum_scatter(out_all, "tensor", scatter_dimension=0, tiled=True)
    out_sum = exchange(out_sum.reshape(n_expert, here, cap, width))
    normed_one_grad = own_back[2] + rest_back[2]

    side = at_expert % 2

    def pair_sum(weight_parts):
        groups = weight_parts.shape[2]
        parts = weight_parts.reshape(blocks, groups, n_expert // blocks, strip, width)
        parts = jnp.swapaxes(parts, 1, 2).reshape(n_expert // 2, 2, groups, strip, width)
        kept = lax.dynamic_index_in_dim(parts, side, 1, keepdims=False)
        given = lax.dynamic_index_in_dim(parts, 1 - side, 1, keepdims=False)
        given = lax.ppermute(given, "expert", [(i, i ^ 1) for i in range(n_expert)])
        return (kept.astype(F32) + given.astype(F32)).astype(BF)

    def plane_sum(parts):
        parts = lax.all_to_all(
            parts,
            "expert",
            split_axis=0,
            concat_axis=0,
            tiled=True,
            axis_index_groups=[list(range(i, n_expert, 2)) for i in range(2)],
        )
        return jnp.sum(parts.astype(F32), axis=0).astype(BF)

    parts = [pair_sum(own_back[0]), pair_sum(rest_back[0])]
    parts = [plane_sum(part) for part in parts]
    parts = [part[i] for part in parts for i in range(part.shape[0])]
    table_grad = ordered(table_back, (own_back[1], rest_back[1]), buckets, count)
    input_norm_grad, gain_one_grad = jax.vjp(rms_scale, inputs_f, gain_one)[1](own_rows(normed_one_grad))
    input_grad = resid_grad + input_norm_grad

    table_grad = relative(table_grad.T.reshape(n_tensor, rel_table.shape[1], count), 0) / share
    small = [router_grad.T, gain_one_grad, gain_two_grad, table_grad, jnp.stack([balance_part, zloss_part])]
    router_total, gain_one_total, gain_two_total, table_total, loss_total = everywhere(small)
    strip_grad = ordered(add, parts[0], *[swap(parts[i], i) for i in steps[1:]], after=(gain_one_total,))
    if share > 1:
        strip_grad = (strip_grad.astype(F32) / share).astype(BF)
    output = home(0, out_sum, (resid,), BF)

    attn_w_grad = lax.all_gather(strip_grad, "expert", axis=0, tiled=True).astype(F32)
    table_total = lax.dynamic_index_in_dim(table_total, at_tensor, 0, keepdims=False).T
    return (
        output,
        input_grad,
        gain_one_total,
        attn_w_grad[:head_cols].T,
        attn_w_grad[head_cols : 2 * head_cols].T,
        attn_w_grad[2 * head_cols : 3 * head_cols].T,
        attn_w_grad[3 * head_cols :],
        table_total,
        gain_two_total,
        router_total.T,
        jnp.swapaxes(gate_grad, 1, 2),
        jnp.swapaxes(up_grad, 1, 2),
        down_grad,
        loss_total,
    )


def solution(mesh):
    return jax.shard_map(
        functools.partial(body, mesh.shape["expert"], mesh.shape["tensor"]),
        mesh=mesh,
        in_specs=(
            P(("expert", "tensor"), None),
            P(),
            P(None, "tensor"),
            P(None, "tensor"),
            P(None, "tensor"),
            P("tensor", None),
            P(None, "tensor"),
            P(),
            P(),
            P("expert", None, "tensor"),
            P("expert", None, "tensor"),
            P("expert", "tensor", None),
            P(),
            P(),
            P(("expert", "tensor"), None),
        ),
        out_specs=(
            P(("expert", "tensor"), None),
            P(("expert", "tensor"), None),
            P(),
            P(None, "tensor"),
            P(None, "tensor"),
            P(None, "tensor"),
            P("tensor", None),
            P(None, "tensor"),
            P(),
            P(),
            P("expert", None, "tensor"),
            P("expert", None, "tensor"),
            P("expert", "tensor", None),
            P(),
        ),
        check_vma=False,
    )
```

```python
import functools

import jax
import jax.numpy as jnp
from jax import lax
from jax.experimental import pallas as pl
from jax.experimental.pallas import tpu as pltpu
from jax.sharding import PartitionSpec as P

HEAD_DIM = 64
TOP = 2
LANES = 128
MIB = 2**20

epsilon = 1e-06
balance_weight = 0.01
zloss_weight = 0.001
highest = lax.Precision.HIGHEST

BF = jnp.bfloat16
F32 = jnp.float32
NN = (((1,), (0,)), ((), ()))
NT = (((1,), (1,)), ((), ()))
TN = (((0,), (0,)), ((), ()))


def dot(left, right, dims=NN):
    return lax.dot_general(left, right, dims, preferred_element_type=F32)


def rms_scale(rows_in, gain):
    inverse = lax.rsqrt(jnp.mean(rows_in * rows_in, axis=-1, keepdims=True) + epsilon)
    return rows_in * inverse * gain


def drop(kernel, at, count):
    def run(*refs):
        kernel(*refs[:at], *refs[at + count :])

    return run


def launch(kernel, operands, after, *, grid, in_specs, out_specs, out_shape, name, flops, scratch=(), moved=0):
    held = [value for value in after if value is not None]
    sizes = [jax.ShapeDtypeStruct(v.shape, v.dtype) for v in operands] + jax.tree.leaves(out_shape)
    moved = moved or sum(v.size * v.dtype.itemsize for v in sizes)
    return pl.pallas_call(
        drop(kernel, len(operands), len(held)),
        grid=grid,
        in_specs=list(in_specs) + [pl.BlockSpec(memory_space=pl.ANY)] * len(held),
        out_specs=out_specs,
        out_shape=out_shape,
        scratch_shapes=scratch,
        compiler_params=pltpu.CompilerParams(vmem_limit_bytes=58 * MIB),
        cost_estimate=pl.CostEstimate(flops=flops, bytes_accessed=moved, transcendentals=0),
        name=name,
    )(*operands, *held)


def lookup(row, index):
    table = jnp.broadcast_to(row, (index.shape[0], LANES))
    parts = [
        jnp.take_along_axis(table, index[:, at : at + LANES], axis=1)
        for at in range(0, index.shape[1], LANES)
    ]
    return jnp.concatenate(parts, axis=1)


def attend_kernel(x_ref, w_ref, bucket_ref, table_ref, qkv_ref, mixed_ref, prob_ref, out_ref):
    seq = x_ref.shape[0]
    tile = 128
    low = lax.broadcasted_iota(jnp.int32, (tile, LANES), 1) < HEAD_DIM
    for part in range(3):
        qkv_ref[part] = dot(x_ref[...], w_ref[part, 0, 0], NT).astype(BF)
    for start in range(0, seq, tile):
        rows = pl.ds(start, tile)
        query = qkv_ref[0, rows, :]
        mixed = []
        for head in range(2):
            part = jnp.where(low if head == 0 else ~low, query, jnp.zeros_like(query))
            scores = dot(part, qkv_ref[1], NT) * 0.125 + lookup(
                table_ref[0, head : head + 1, :], bucket_ref[rows, :]
            )
            scores = jnp.exp(scores - jnp.max(scores, axis=-1, keepdims=True))
            weights = (scores / jnp.sum(scores, axis=-1, keepdims=True)).astype(BF)
            prob_ref[head, rows, :] = weights
            mixed.append(dot(weights, qkv_ref[2]))
        mixed_ref[rows, :] = jnp.where(low, mixed[0], mixed[1]).astype(BF)
    out = dot(mixed_ref[...], w_ref[3, 0, 0])

    @pl.when(pl.program_id(0) == 0)
    def _():
        out_ref[...] = out

    @pl.when(pl.program_id(0) > 0)
    def _():
        out_ref[...] += out


def attend(x, weights, buckets, table, after):
    seq, width = x.shape
    _, pairs, groups, _, _ = weights.shape
    steps = pairs * groups
    full = pl.BlockSpec((seq, width), lambda i: (0, 0))
    col = pl.BlockSpec((seq, LANES), lambda i: (0, i))
    return launch(
        attend_kernel,
        (x, weights, buckets, table),
        after,
        grid=(steps,),
        in_specs=[
            full,
            pl.BlockSpec((4, 1, 1, LANES, width), lambda i: (0, i % pairs, i // pairs, 0, 0)),
            pl.BlockSpec((seq, seq), lambda i: (0, 0)),
            pl.BlockSpec((1, 2, LANES), lambda i: (i, 0, 0)),
        ],
        out_specs=[
            pl.BlockSpec((3, seq, LANES), lambda i: (0, 0, i)),
            col,
            pl.BlockSpec((2, seq, seq), lambda i: (i, 0, 0)),
            full,
        ],
        out_shape=[
            jax.ShapeDtypeStruct((3, seq, steps * LANES), BF),
            jax.ShapeDtypeStruct((seq, steps * LANES), BF),
            jax.ShapeDtypeStruct((2 * steps, seq, seq), BF),
            jax.ShapeDtypeStruct((seq, width), F32),
        ],
        name="attend",
        flops=steps * seq * LANES * 2 * (4 * width + 4 * seq),
    )


def attend_back_kernel(
    x_ref, grad_ref, w_ref, qkv_ref, mixed_ref, prob_ref, weight_ref, score_ref, normed_ref, part_ref
):
    seq = x_ref.shape[0]
    tile = 128
    low = lax.broadcasted_iota(jnp.int32, (tile, LANES), 1) < HEAD_DIM
    mixed_grad = dot(grad_ref[...], w_ref[3, 0, 0], NT).astype(BF)
    part_ref[...] = mixed_grad
    queries = []
    for start in range(0, seq, tile):
        rows = pl.ds(start, tile)
        grad = part_ref[rows, :]
        back = []
        for head in range(2):
            part = jnp.where(low if head == 0 else ~low, grad, jnp.zeros_like(grad))
            weights = prob_ref[head, rows, :].astype(F32)
            weight_grad = dot(part, qkv_ref[2], NT)
            score = weights * (
                weight_grad - jnp.sum(weights * weight_grad, axis=-1, keepdims=True)
            )
            score = score.astype(BF)
            score_ref[head, rows, :] = score
            back.append(dot(score, qkv_ref[1]))
        queries.append((jnp.where(low, back[0], back[1]) * 0.125).astype(BF))
    wide = lax.broadcasted_iota(jnp.int32, (seq, LANES), 1) < HEAD_DIM
    keys = [dot(score_ref[head], qkv_ref[0], TN) for head in range(2)]
    vals = [dot(prob_ref[head], mixed_grad, TN) for head in range(2)]
    back = jnp.concatenate(
        [
            jnp.concatenate(queries, 0),
            (jnp.where(wide, keys[0], keys[1]) * 0.125).astype(BF),
            jnp.where(wide, vals[0], vals[1]).astype(BF),
        ],
        1,
    )
    weight_ref[:3, 0, 0] = dot(back, x_ref[...], TN).reshape(3, LANES, -1).astype(BF)
    weight_ref[3, 0, 0] = dot(mixed_ref[...], grad_ref[...], TN).astype(BF)
    normed = dot(back, w_ref[:3, 0, 0].reshape(3 * LANES, -1))

    @pl.when(pl.program_id(0) == 0)
    def _():
        normed_ref[...] = normed

    @pl.when(pl.program_id(0) > 0)
    def _():
        normed_ref[...] += normed


def attend_back(x, grad, weights, qkv, mixed, probs, after):
    seq, width = x.shape
    _, pairs, groups, _, _ = weights.shape
    steps = pairs * groups
    full = pl.BlockSpec((seq, width), lambda i: (0, 0))
    col = pl.BlockSpec((seq, LANES), lambda i: (0, i))
    strip = pl.BlockSpec((4, 1, 1, LANES, width), lambda i: (0, i % pairs, i // pairs, 0, 0))
    square = pl.BlockSpec((2, seq, seq), lambda i: (i, 0, 0))
    return launch(
        attend_back_kernel,
        (x, grad, weights, qkv, mixed, probs),
        after,
        grid=(steps,),
        in_specs=[full, full, strip, pl.BlockSpec((3, seq, LANES), lambda i: (0, 0, i)), col, square],
        out_specs=[strip, square, full],
        out_shape=[
            jax.ShapeDtypeStruct((4, pairs, groups, LANES, width), BF),
            jax.ShapeDtypeStruct(probs.shape, BF),
            jax.ShapeDtypeStruct((seq, width), F32),
        ],
        scratch=[pltpu.VMEM((seq, LANES), BF)],
        name="attend_back",
        flops=steps * seq * LANES * 2 * (8 * width + 8 * seq),
    )


def table_kernel(*refs):
    *score_refs, bucket_ref, out_ref = refs
    marks = bucket_ref[...]
    tile, seq = marks.shape
    count = out_ref.shape[1] // tile
    ids = lax.broadcasted_iota(jnp.int32, (tile, count, seq), 1)
    onehot = (jnp.broadcast_to(marks[:, None, :], ids.shape) == ids).astype(F32)
    onehot = onehot.astype(BF).reshape(tile * count, seq)
    block = jnp.concatenate([ref[...].reshape(-1, seq) for ref in score_refs], 0)
    sums = dot(block, onehot, NT)

    @pl.when(pl.program_id(0) == 0)
    def _():
        out_ref[...] = sums

    @pl.when(pl.program_id(0) > 0)
    def _():
        out_ref[...] += sums


def table_back(scores, buckets, count, after):
    heads = sum(part.shape[0] for part in scores)
    seq = buckets.shape[0]
    tile = 16
    sums = launch(
        table_kernel,
        (*scores, buckets),
        after,
        grid=(seq // tile,),
        in_specs=[pl.BlockSpec((part.shape[0], tile, seq), lambda i: (0, i, 0)) for part in scores]
        + [pl.BlockSpec((tile, seq), lambda i: (i, 0))],
        out_specs=pl.BlockSpec((heads * tile, tile * count), lambda i: (0, 0)),
        out_shape=jax.ShapeDtypeStruct((heads * tile, tile * count), F32),
        name="table_back",
        flops=heads * tile * seq * seq * count * 2 * 4,
    )
    sums = sums.reshape(heads, tile, tile, count)
    same = jnp.eye(tile, dtype=F32)[None, :, :, None]
    return jnp.sum(sums * same, axis=(1, 2)).T


def assemble(place, halves, after):
    sources, groups, strip, _ = halves[0].shape
    width = sum(half.shape[3] for half in halves)
    held = [value for value in after if value is not None]

    def kernel(place_ref, *refs):
        refs[-1][0] = jnp.concatenate([ref[0] for ref in refs[: len(halves)]], -1)

    return pl.pallas_call(
        kernel,
        grid_spec=pltpu.PrefetchScalarGridSpec(
            num_scalar_prefetch=1,
            grid=(sources,),
            in_specs=[
                pl.BlockSpec((1, groups, strip, half.shape[3]), lambda i, at, side=side: (at[side, i], 0, 0, 0))
                for side, half in enumerate(halves)
            ]
            + [pl.BlockSpec(memory_space=pl.ANY)] * len(held),
            out_specs=pl.BlockSpec((1, groups, strip, width), lambda i, at: (i, 0, 0, 0)),
        ),
        out_shape=jax.ShapeDtypeStruct((sources, groups, strip, width), BF),
        cost_estimate=pl.CostEstimate(flops=0, bytes_accessed=4 * sources * groups * strip * width, transcendentals=0),
        name="assemble",
    )(place, *halves, *held)


def split_kernel(in_ref, *out_refs):
    cols = in_ref.shape[0] // 4
    for part, ref in enumerate(out_refs):
        rows = in_ref[part * cols : (part + 1) * cols, :].astype(F32)
        ref[...] = rows if part == 3 else rows.T


def split(value, after):
    rows, width = value.shape
    cols = rows // 4
    tile = min(width, 256)
    wide = pl.BlockSpec((tile, cols), lambda i: (i, 0))
    return launch(
        split_kernel,
        (value,),
        after,
        grid=(width // tile,),
        in_specs=[pl.BlockSpec((rows, tile), lambda i: (0, i))],
        out_specs=[wide, wide, wide, pl.BlockSpec((cols, tile), lambda i: (0, i))],
        out_shape=[jax.ShapeDtypeStruct((width, cols), F32)] * 3 + [jax.ShapeDtypeStruct((cols, width), F32)],
        name="split",
        flops=value.size,
    )


def copy_kernel(from_ref, to_ref):
    to_ref[...] = from_ref[...]


def hold(value, after):
    full = pl.BlockSpec(value.shape, lambda i: (0,) * value.ndim)
    return launch(
        copy_kernel,
        (value,),
        after,
        grid=(1,),
        in_specs=[full],
        out_specs=full,
        out_shape=jax.ShapeDtypeStruct(value.shape, value.dtype),
        name="hold",
        flops=0,
    )


def stack(place, parts, after):
    shape = parts[0].shape
    held = [value for value in after if value is not None]
    count = len(parts)

    def kernel(place_ref, *refs):
        for i in range(count):

            @pl.when(pl.program_id(0) == i)
            def _():
                refs[-1][...] = refs[i][...]

    full = pl.BlockSpec(shape, lambda s, at: (0,) * len(shape))
    return pl.pallas_call(
        kernel,
        grid_spec=pltpu.PrefetchScalarGridSpec(
            num_scalar_prefetch=1,
            grid=(count,),
            in_specs=[full] * count + [pl.BlockSpec(memory_space=pl.ANY)] * len(held),
            out_specs=pl.BlockSpec(shape, lambda s, at: (at[s],) + (0,) * (len(shape) - 1)),
        ),
        out_shape=jax.ShapeDtypeStruct((count * shape[0],) + shape[1:], BF),
        compiler_params=pltpu.CompilerParams(vmem_limit_bytes=58 * MIB),
        name="stack",
    )(place, *parts, *held)


def sum_kernel(*refs):
    *parts, out_ref = refs
    total = parts[0][...].astype(F32)
    for ref in parts[1:]:
        total += ref[...].astype(F32)
    out_ref[...] = total.astype(out_ref.dtype)


def add(*operands):
    *parts, after = operands
    shape = parts[0].shape
    if parts[0].ndim > 2:
        block = pl.BlockSpec((1,) + shape[1:], lambda i: (i,) + (0,) * (len(shape) - 1))
    else:
        block = pl.BlockSpec(shape, lambda i: (0, 0))
    return launch(
        sum_kernel,
        parts,
        after,
        grid=(shape[0] if len(shape) > 2 else 1,),
        in_specs=[block] * len(parts),
        out_specs=block,
        out_shape=jax.ShapeDtypeStruct(shape, parts[0].dtype),
        name="add",
        flops=parts[0].size,
    )


def dispatch_kernel(id_ref, x_ref, out_ref):
    count = out_ref.shape[0]
    slot = lax.broadcasted_iota(jnp.int32, (count, x_ref.shape[0]), 0) + pl.program_id(0) * count
    onehot = (slot == id_ref[0:1, :]) | (slot == id_ref[1:2, :])
    out_ref[...] = dot(onehot.astype(F32).astype(BF), x_ref[...]).astype(BF)


def to_slots(ids, value, slots, after):
    rows, width = value.shape
    steps = 4
    return launch(
        dispatch_kernel,
        (ids, value),
        after,
        grid=(steps,),
        in_specs=[
            pl.BlockSpec((TOP, rows), lambda i: (0, 0)),
            pl.BlockSpec((rows, width), lambda i: (0, 0)),
        ],
        out_specs=pl.BlockSpec((slots // steps, width), lambda i: (i, 0)),
        out_shape=jax.ShapeDtypeStruct((slots, width), BF),
        name="to_slots",
        flops=slots * rows * width * 2,
    )


def to_many_slots(place, ids, values, here, after):
    chunks = place.shape[0]
    _, rows, width = values.shape
    count = here[0] * here[1]
    held = [value for value in after if value is not None]
    steps = 4
    part = here[0] // steps

    def kernel(place_ref, id_ref, x_ref, *refs):
        out_ref = refs[-1]
        total = part * here[1]
        slot = lax.broadcasted_iota(jnp.int32, (total, rows), 0) + pl.program_id(1) * total
        onehot = (slot == id_ref[0, 0:1, :]) | (slot == id_ref[0, 1:2, :])
        out = dot(onehot.astype(F32).astype(BF), x_ref[0])
        out_ref[...] = out.reshape(out_ref.shape).astype(BF)

    return pl.pallas_call(
        kernel,
        grid_spec=pltpu.PrefetchScalarGridSpec(
            num_scalar_prefetch=1,
            grid=(chunks, steps),
            in_specs=[
                pl.BlockSpec((1, TOP, rows), lambda c, j, at: (c, 0, 0)),
                pl.BlockSpec((1, rows, width), lambda c, j, at: (at[c], 0, 0)),
            ]
            + [pl.BlockSpec(memory_space=pl.ANY)] * len(held),
            out_specs=pl.BlockSpec((part, 1, here[1], width), lambda c, j, at: (j, c, 0, 0)),
        ),
        out_shape=jax.ShapeDtypeStruct((here[0], chunks, here[1], width), BF),
        compiler_params=pltpu.CompilerParams(vmem_limit_bytes=40 * MIB),
        cost_estimate=pl.CostEstimate(
            flops=2 * chunks * count * rows * width, bytes_accessed=4 * chunks * count * width, transcendentals=0
        ),
        name="to_many_slots",
    )(place, ids, values, *held)


def collect_kernel(id_ref, slot_ref, *refs):
    *more, out_ref = refs
    rows = out_ref.shape[0]
    slot = lax.broadcasted_iota(jnp.int32, (rows, slot_ref.shape[0]), 1)
    onehot = (slot == id_ref[:, 0:1]) | (slot == id_ref[:, 1:2])
    total = dot(onehot.astype(F32).astype(BF), slot_ref[...])
    for ref in more:
        total += ref[...].astype(F32)
    out_ref[...] = total.astype(out_ref.dtype)


def to_tokens(ids, slots, more, kind, after):
    rows = ids.shape[0]
    count, width = slots.shape
    steps = 2
    block = pl.BlockSpec((rows // steps, width), lambda i: (i, 0))
    return launch(
        collect_kernel,
        (ids, slots, *more),
        after,
        grid=(steps,),
        in_specs=[
            pl.BlockSpec((rows // steps, TOP), lambda i: (i, 0)),
            pl.BlockSpec((count, width), lambda i: (0, 0)),
        ]
        + [block] * len(more),
        out_specs=block,
        out_shape=jax.ShapeDtypeStruct((rows, width), kind),
        name="to_tokens",
        flops=count * rows * width * 2,
    )


def flat(ref):
    block = ref[...]
    return block.astype(F32).reshape(-1, block.shape[-1]).astype(BF)


def expert_kernel(
    base_ref,
    x_ref,
    g_ref,
    other_ref,
    gate_ref,
    up_ref,
    down_ref,
    router_ref,
    out_ref,
    back_ref,
    hidden_ref,
    gate_back_ref,
    up_back_ref,
    route_ref,
):
    expert = pl.program_id(0)
    x = flat(x_ref)
    g = flat(g_ref)
    lanes = lax.broadcasted_iota(jnp.int32, (x.shape[0], LANES), 1)
    sign = (lanes == base_ref[0] + expert).astype(F32) - (lanes == other_ref[0]).astype(F32)
    logits = dot(x, router_ref[...])
    apart = jnp.sum(sign * (logits[:, :LANES] + logits[:, LANES:]), axis=-1, keepdims=True)
    weight = 1.0 / (1.0 + jnp.exp(-apart))
    gate = dot(x, gate_ref[0], NT)
    up = dot(x, up_ref[0], NT)
    grad = dot(g, down_ref[0], NT)
    scale = 0.7978845608028654
    square = gate * gate
    bent = jnp.tanh(scale * gate * (1.0 + 0.044715 * square))
    half = 0.5 + 0.5 * bent
    act = gate * half
    slope = half + 0.5 * gate * (1.0 - bent * bent) * (scale + 3 * 0.044715 * scale * square)
    hidden = act * up
    mark = weight * (1.0 - weight) * jnp.sum(hidden * grad, axis=-1, keepdims=True)
    mark = (mark * sign).astype(BF)
    grad = grad * weight
    up_back = (grad * act).astype(BF)
    gate_back = (grad * up * slope).astype(BF)
    hidden_ref[0] = (hidden * weight).astype(BF)
    gate_back_ref[0] = gate_back
    up_back_ref[0] = up_back
    out = dot(hidden.astype(BF), down_ref[0]) * weight
    out_ref[...] = out.reshape(out_ref.shape).astype(BF)
    back = dot(gate_back, gate_ref[0]) + dot(up_back, up_ref[0])
    back += dot(mark, router_ref[:, :LANES], NT)
    back_ref[...] = back.reshape(back_ref.shape).astype(BF)
    part = dot(mark, x, TN)

    @pl.when(expert == 0)
    def _():
        route_ref[...] = jnp.zeros_like(route_ref)

    route_ref[...] += part


def chunk_spec(array, chunk):
    sources, _, _, slots, width = array.shape
    return pl.BlockSpec((sources, 1, 1, slots, width), lambda e: (0, chunk, e, 0, 0))


def expert_chunk(base, x_at, g_at, other, gate_w, up_w, down_w, router_pair, after):
    (x, x_chunk), (g, g_chunk) = x_at, g_at
    sources, _, here, slots, width = x.shape
    hidden = down_w.shape[1]
    count = sources * slots
    rows = pl.BlockSpec((sources, 1, slots, width), lambda e: (0, e, 0, 0))
    middle = pl.BlockSpec((1, count, hidden), lambda e: (e, 0, 0))
    weights = pl.BlockSpec((1, hidden, width), lambda e: (e, 0, 0))
    return launch(
        expert_kernel,
        (base, x, g, other, gate_w, up_w, down_w, router_pair),
        after,
        grid=(here,),
        in_specs=[
            pl.BlockSpec(memory_space=pltpu.SMEM),
            chunk_spec(x, x_chunk),
            chunk_spec(g, g_chunk),
            pl.BlockSpec((1, count, 1), lambda e: (e, 0, 0)),
            weights,
            weights,
            weights,
            pl.BlockSpec((width, 2 * LANES), lambda e: (0, 0)),
        ],
        out_specs=[rows, rows, middle, middle, middle, pl.BlockSpec((LANES, width), lambda e: (0, 0))],
        out_shape=[jax.ShapeDtypeStruct((sources, here, slots, width), BF)] * 2
        + [jax.ShapeDtypeStruct((here, count, hidden), BF)] * 3
        + [jax.ShapeDtypeStruct((LANES, width), F32)],
        name="experts",
        flops=12 * here * count * width * hidden * 2,
    )


def weight_kernel(*refs, chunks):
    xs, gs, hidden, gates, ups = (refs[i * chunks : (i + 1) * chunks] for i in range(5))
    gate_ref, up_ref, down_ref = refs[5 * chunks :]
    x = jnp.concatenate([flat(ref) for ref in xs], 0)
    gate_ref[0] = dot(jnp.concatenate([ref[0] for ref in gates], 0), x, TN)
    up_ref[0] = dot(jnp.concatenate([ref[0] for ref in ups], 0), x, TN)
    g = jnp.concatenate([flat(ref) for ref in gs], 0)
    down_ref[0] = dot(jnp.concatenate([ref[0] for ref in hidden], 0), g, TN)


def weight_grads(xs, gs, hidden, gates, ups, after):
    sources, _, here, slots, width = xs[0][0].shape
    depth = hidden[0].shape[2]
    middle = pl.BlockSpec((1, sources * slots, depth), lambda e: (e, 0, 0))
    chunks = len(xs)
    return launch(
        functools.partial(weight_kernel, chunks=chunks),
        (*[v for v, _ in xs], *[v for v, _ in gs], *hidden, *gates, *ups),
        after,
        grid=(here,),
        in_specs=[chunk_spec(*v) for v in (*xs, *gs)] + [middle] * (3 * chunks),
        out_specs=[pl.BlockSpec((1, depth, width), lambda e: (e, 0, 0))] * 3,
        out_shape=[jax.ShapeDtypeStruct((here, depth, width), F32)] * 3,
        name="expert_weight_grads",
        flops=4 * here * chunks * sources * slots * width * depth * 2,
    )


def body(
    n_expert,
    n_tensor,
    inputs,
    gain_one,
    w_query,
    w_key,
    w_value,
    w_out,
    rel_table,
    gain_two,
    router,
    w_gate,
    w_up,
    w_down,
    routes,
    buckets,
    grad_out,
):
    rows, width = inputs.shape
    experts = router.shape[1]
    here = w_gate.shape[0]
    tokens = routes.shape[0]
    cap = (5 * rows * TOP + 4 * experts - 1) // (4 * experts)
    slots = experts * cap
    seq = buckets.shape[0]
    share = seq // rows
    count = rel_table.shape[0]
    head_cols = w_query.shape[1]
    at_expert = lax.axis_index("expert")
    at_tensor = lax.axis_index("tensor")
    steps = range(n_tensor)
    far = range(2, n_tensor)
    last = [None]

    def swap(value, step):
        return lax.ppermute(value, "tensor", [(i, i ^ step) for i in range(n_tensor)])

    def exchange(value):
        return lax.all_to_all(value, "expert", split_axis=0, concat_axis=0, tiled=True)

    def ordered(run, *operands, after=()):
        before = last[0] if isinstance(last[0], tuple) else (last[0],)
        result = run(*operands, (*before, *after))
        last[0] = result[0] if isinstance(result, (list, tuple)) else result
        return result

    labels = jnp.arange(experts, dtype=jnp.int32)
    grouped = routes.T.reshape(TOP, n_expert * n_tensor, rows)
    marks = (grouped[:, :, None, :] == labels[:, None]).astype(BF)
    order = jnp.arange(rows, dtype=jnp.int32)
    earlier = (order[:, None] < order[None, :]).astype(BF)
    ahead = jnp.einsum("kges,st->kget", marks, earlier, preferred_element_type=F32)
    first_count = jnp.sum(marks[0].astype(F32), axis=-1, keepdims=True)
    ahead = ahead + jnp.stack([jnp.zeros_like(first_count), first_count])
    places = jnp.sum(ahead * marks.astype(F32), axis=2).astype(jnp.int32)
    slot_ids = jnp.where(places < cap, grouped * cap + places, -1)
    slot_ids = slot_ids.reshape(TOP, n_expert, n_tensor, rows)
    choices = grouped.reshape(TOP, n_expert, n_tensor, rows)

    def relative(value, axis):
        return jnp.stack([lax.dynamic_index_in_dim(value, at_tensor ^ i, axis, keepdims=False) for i in steps])

    own_ids = relative(lax.dynamic_index_in_dim(slot_ids, at_expert, 1, keepdims=False), 1)
    id_rows = [own_ids[i] for i in steps]
    id_cols = jnp.swapaxes(own_ids, 1, 2)
    local = slot_ids - at_expert * (here * cap)
    slot_here = jnp.arange(here * cap, dtype=jnp.int32)[:, None]
    partner = jnp.sum(
        jnp.where(local[0][:, :, None, :] == slot_here, choices[1][:, :, None, :], 0)
        + jnp.where(local[1][:, :, None, :] == slot_here, choices[0][:, :, None, :], 0),
        axis=-1,
    ).reshape(n_expert, n_tensor, here, cap)
    partners = jnp.swapaxes(relative(partner, 1), 1, 2).reshape(n_tensor, here, n_expert * cap, 1)

    def send(step, value, after=()):
        buffer = ordered(to_slots, id_rows[step], value, slots, after=after)
        return exchange(buffer.reshape(n_expert, here, cap, width))

    def home(step, value, more=(), kind=BF, after=()):
        return ordered(to_tokens, id_cols[step], value.reshape(slots, width), more, kind, after=after)

    def gather(value):
        whole = lax.all_gather(value, "tensor", axis=0, tiled=True).reshape(n_tensor, rows, width)
        return [lax.dynamic_index_in_dim(whole, at_tensor ^ i, 0, keepdims=False) for i in steps]

    def everywhere(values):
        total = jnp.concatenate([value.reshape(-1) for value in values])
        for axis, size in (("expert", n_expert), ("tensor", n_tensor)):
            for bit in range(size.bit_length() - 1):
                total = total + lax.ppermute(total, axis, [(i, i ^ (1 << bit)) for i in range(size)])
        totals = []
        for value in values:
            totals.append(total[: value.size].reshape(value.shape))
            total = total[value.size :]
        return totals

    def whole_seq(value):
        if share == 1:
            return value
        groups = [[i * share + j for j in range(share)] for i in range(n_tensor // share)]
        return lax.all_gather(value, "tensor", axis=0, tiled=True, axis_index_groups=groups)

    def own_rows(value):
        if share == 1:
            return value
        return lax.dynamic_slice_in_dim(value, (at_tensor % share) * rows, rows, 0)

    packed = jnp.concatenate([w_query.T, w_key.T, w_value.T, w_out], 0)
    strip = 4 * head_cols // n_expert
    blocks = 4 * head_cols // LANES
    pairs = blocks // 4
    own_w = packed.reshape(4, pairs, 1, LANES, width)
    packed = ordered(hold, lax.dynamic_slice_in_dim(packed, at_expert * strip, strip, 0))
    strips = jnp.stack([swap(packed, i) for i in steps[1:]])
    table_own = jnp.pad(rel_table.T, ((0, 0), (0, LANES - count)))
    table_all = jnp.stack([table_own] + [swap(table_own, i) for i in steps[1:]])
    table_all = table_all.reshape(n_tensor * pairs, 2, LANES)

    inputs_f = inputs.astype(F32)
    normed_one = rms_scale(inputs_f, gain_one).astype(BF)
    attn_in = whole_seq(normed_one)
    grad_low = ordered(hold, grad_out, after=(strips, table_all))
    grad_all = lax.all_gather(grad_low, "tensor", axis=0, tiled=True).reshape(n_tensor, rows, width)
    own_part = ordered(attend, attn_in, own_w, buckets, table_all[:pairs])

    bits = [1 << i for i in range(1, n_expert.bit_length() - 1)]
    sources = jnp.arange(n_expert, dtype=jnp.int32) ^ at_expert
    halves, places, came = [], [], []
    for half in range(2):
        held, order = strips[None, :, :, half * width // 2 : (half + 1) * width // 2], [0]
        for bit in (bits if half == 0 else bits[::-1]) + [1]:
            came.append(held)
            held = jnp.concatenate([held, lax.ppermute(held, "expert", [(i, i ^ bit) for i in range(n_expert)])], 0)
            order = order + [i ^ bit for i in order]
        halves.append(held)
        where = jnp.asarray([order.index(i) for i in range(n_expert)], jnp.int32)
        places.append(jnp.sum(jnp.where(sources[:, None] == jnp.arange(n_expert), where, 0), 1))
    places = jnp.stack(places).astype(jnp.int32)

    grad_own = send(0, grad_out, (came[len(bits)], came[-1]))
    attn_w = ordered(assemble, places, halves)
    others = jnp.arange(1, n_tensor, dtype=jnp.int32) ^ at_tensor
    grad_rest = exchange(
        ordered(to_many_slots, others, own_ids[1:], grad_all, (n_expert, here * cap), after=(grad_own,))
    )
    grad_slots = {0: (grad_own, 0)} | {i: (grad_rest, i - 1) for i in steps[1:]}
    attn_w = attn_w.reshape(blocks, n_expert // blocks, n_tensor - 1, strip, width)
    attn_w = jnp.swapaxes(attn_w, 1, 2).reshape(4, pairs, n_tensor - 1, LANES, width)
    rest_part = ordered(attend, attn_in, attn_w, buckets, table_all[pairs:])
    resid = inputs_f + own_rows(own_part[3] + rest_part[3])
    normed_two = rms_scale(resid, gain_two)
    normed_low = normed_two.astype(BF)

    token_far = gather(normed_low)
    token_slots = {0: send(0, normed_low, (grad_rest,))}

    counts = jnp.sum((routes.T[:, None, :] == labels[:, None]).astype(F32), axis=(0, 2))
    route_share = counts / (tokens * TOP)

    def losses(normed, router_w):
        logits = jnp.dot(normed, router_w, precision=highest)
        router_probs = jax.nn.softmax(logits, axis=-1)
        log_totals = jax.nn.logsumexp(logits, axis=-1)
        balance = experts * jnp.sum(route_share * jnp.sum(router_probs, axis=0)) / tokens
        return balance, jnp.sum(log_totals * log_totals) / tokens

    (balance_part, zloss_part), losses_back = jax.vjp(losses, normed_two, router)
    normed_grad, router_grad = losses_back(
        (jnp.asarray(balance_weight, F32), jnp.asarray(zloss_weight, F32))
    )

    router_high = router.astype(BF)
    router_low = (router - router_high.astype(F32)).astype(BF)
    fill = ((0, 0), (0, LANES - experts))
    router_pair = jnp.concatenate([jnp.pad(router_high, fill), jnp.pad(router_low, fill)], 1)
    base = jnp.full((1,), at_expert * here, jnp.int32)
    gate_w = jnp.swapaxes(w_gate, 1, 2)
    up_w = jnp.swapaxes(w_up, 1, 2)

    def rows_in(value):
        value, chunk = value
        if cap % 8 == 0:
            return value.reshape(n_expert, -1, here, cap, width), chunk
        value = value.reshape(n_expert, -1, here, cap, width)[:, chunk]
        return jnp.swapaxes(value, 0, 1).reshape(1, 1, here, n_expert * cap, width), 0

    def rows_out(value):
        if cap % 8 == 0:
            return value
        return jnp.swapaxes(value.reshape(here, n_expert, cap, width), 0, 1)

    xs, gs, done = {}, {}, {}

    def work(step):
        xs[step], gs[step] = rows_in((token_slots[step], 0)), rows_in(grad_slots[step])
        done[step] = ordered(
            expert_chunk, base, xs[step], gs[step], partners[step], gate_w, up_w, w_down, router_pair
        )

    token_slots[1] = send(1, token_far[1])
    work(0)
    for i in far:
        token_slots[i] = send(i, token_far[i])
        work(i - 1)
    work(n_tensor - 1)
    backs = {i: rows_out(done[i][1]) for i in steps}
    outs = {i: rows_out(done[i][0]) for i in steps}
    moe_far, near = [], None
    for i in far:
        moe_far.append(swap(home(i, exchange(backs[i]), after=moe_far[-1:]), i))
        if i == far[0]:
            near = exchange(ordered(add, backs[0], swap(backs[1], 1)))
    gate_grad, up_grad, down_grad = ordered(
        weight_grads,
        *[[v[i] for i in steps] for v in (xs, gs)],
        *[[done[i][j] for i in steps] for j in (2, 3, 4)],
    )
    moe_grad = home(0, near, moe_far, F32)
    router_grad = router_grad + sum(done[i][5] for i in steps)[:experts].T

    grad_f = grad_out.astype(F32)
    resid_norm_grad, gain_two_grad = jax.vjp(rms_scale, resid, gain_two)[1](normed_grad + moe_grad)
    resid_grad = grad_f + resid_norm_grad
    attn_grad = whole_seq(resid_grad.astype(BF))
    out_all = ordered(stack, jnp.arange(n_tensor, dtype=jnp.int32) ^ at_tensor, [outs[i] for i in steps])
    rest_back = ordered(attend_back, attn_in, attn_grad, attn_w, *rest_part[:3])
    own_back = ordered(attend_back, attn_in, attn_grad, own_w, *own_part[:3])
    out_sum = lax.psum_scatter(out_all, "tensor", scatter_dimension=0, tiled=True)
    out_sum = exchange(out_sum.reshape(n_expert, here, cap, width))
    normed_one_grad = own_back[2] + rest_back[2]

    side = at_expert % 2

    def pair_sum(weight_parts):
        groups = weight_parts.shape[2]
        parts = weight_parts.reshape(blocks, groups, n_expert // blocks, strip, width)
        parts = jnp.swapaxes(parts, 1, 2).reshape(n_expert // 2, 2, groups, strip, width)
        kept = lax.dynamic_index_in_dim(parts, side, 1, keepdims=False)
        given = lax.dynamic_index_in_dim(parts, 1 - side, 1, keepdims=False)
        given = lax.ppermute(given, "expert", [(i, i ^ 1) for i in range(n_expert)])
        return (kept.astype(F32) + given.astype(F32)).astype(BF)

    def plane_sum(parts):
        parts = lax.all_to_all(
            parts,
            "expert",
            split_axis=0,
            concat_axis=0,
            tiled=True,
            axis_index_groups=[list(range(i, n_expert, 2)) for i in range(2)],
        )
        return jnp.sum(parts.astype(F32), axis=0).astype(BF)

    parts = [pair_sum(own_back[0]), pair_sum(rest_back[0])]
    parts = [plane_sum(part) for part in parts]
    parts = [part[i] for part in parts for i in range(part.shape[0])]
    table_grad = ordered(table_back, (own_back[1], rest_back[1]), buckets, count)
    input_norm_grad, gain_one_grad = jax.vjp(rms_scale, inputs_f, gain_one)[1](own_rows(normed_one_grad))
    input_grad = resid_grad + input_norm_grad

    table_grad = relative(table_grad.T.reshape(n_tensor, rel_table.shape[1], count), 0) / share
    small = [router_grad.T, gain_one_grad, gain_two_grad, table_grad, jnp.stack([balance_part, zloss_part])]
    router_total, gain_one_total, gain_two_total, table_total, loss_total = everywhere(small)
    strip_grad = ordered(add, parts[0], *[swap(parts[i], i) for i in steps[1:]], after=(gain_one_total,))
    if share > 1:
        strip_grad = (strip_grad.astype(F32) / share).astype(BF)
    output = home(0, out_sum, (resid,), BF)

    attn_w_grad = lax.all_gather(strip_grad, "expert", axis=0, tiled=True)
    query_grad, key_grad, value_grad, out_proj_grad = ordered(split, attn_w_grad)
    table_total = lax.dynamic_index_in_dim(table_total, at_tensor, 0, keepdims=False).T
    return (
        output,
        input_grad,
        gain_one_total,
        query_grad,
        key_grad,
        value_grad,
        out_proj_grad,
        table_total,
        gain_two_total,
        router_total.T,
        jnp.swapaxes(gate_grad, 1, 2),
        jnp.swapaxes(up_grad, 1, 2),
        down_grad,
        loss_total,
    )


def solution(mesh):
    return jax.shard_map(
        functools.partial(body, mesh.shape["expert"], mesh.shape["tensor"]),
        mesh=mesh,
        in_specs=(
            P(("expert", "tensor"), None),
            P(),
            P(None, "tensor"),
            P(None, "tensor"),
            P(None, "tensor"),
            P("tensor", None),
            P(None, "tensor"),
            P(),
            P(),
            P("expert", None, "tensor"),
            P("expert", None, "tensor"),
            P("expert", "tensor", None),
            P(),
            P(),
            P(("expert", "tensor"), None),
        ),
        out_specs=(
            P(("expert", "tensor"), None),
            P(("expert", "tensor"), None),
            P(),
            P(None, "tensor"),
            P(None, "tensor"),
            P(None, "tensor"),
            P("tensor", None),
            P(None, "tensor"),
            P(),
            P(),
            P("expert", None, "tensor"),
            P("expert", None, "tensor"),
            P("expert", "tensor", None),
            P(),
        ),
        check_vma=False,
    )
```

```python
import functools

import jax
import jax.numpy as jnp
from jax import lax
from jax.experimental import pallas as pl
from jax.experimental.pallas import tpu as pltpu
from jax.sharding import PartitionSpec as P

HEAD_DIM = 64
TOP = 2
LANES = 128
MIB = 2**20

epsilon = 1e-06
balance_weight = 0.01
zloss_weight = 0.001
highest = lax.Precision.HIGHEST

BF = jnp.bfloat16
F32 = jnp.float32
NN = (((1,), (0,)), ((), ()))
NT = (((1,), (1,)), ((), ()))
TN = (((0,), (0,)), ((), ()))


def dot(left, right, dims=NN):
    return lax.dot_general(left, right, dims, preferred_element_type=F32)


def rms_scale(rows_in, gain):
    inverse = lax.rsqrt(jnp.mean(rows_in * rows_in, axis=-1, keepdims=True) + epsilon)
    return rows_in * inverse * gain


def drop(kernel, at, count):
    def run(*refs):
        kernel(*refs[:at], *refs[at + count :])

    return run


def launch(kernel, operands, after, *, grid, in_specs, out_specs, out_shape, name, flops, scratch=(), moved=0):
    held = [value for value in after if value is not None]
    sizes = [jax.ShapeDtypeStruct(v.shape, v.dtype) for v in operands] + jax.tree.leaves(out_shape)
    moved = moved or sum(v.size * v.dtype.itemsize for v in sizes)
    return pl.pallas_call(
        drop(kernel, len(operands), len(held)),
        grid=grid,
        in_specs=list(in_specs) + [pl.BlockSpec(memory_space=pl.ANY)] * len(held),
        out_specs=out_specs,
        out_shape=out_shape,
        scratch_shapes=scratch,
        compiler_params=pltpu.CompilerParams(vmem_limit_bytes=58 * MIB),
        cost_estimate=pl.CostEstimate(flops=flops, bytes_accessed=moved, transcendentals=0),
        name=name,
    )(*operands, *held)


def lookup(row, index):
    table = jnp.broadcast_to(row, (index.shape[0], LANES))
    parts = [
        jnp.take_along_axis(table, index[:, at : at + LANES], axis=1)
        for at in range(0, index.shape[1], LANES)
    ]
    return jnp.concatenate(parts, axis=1)


def attend_kernel(x_ref, w_ref, bucket_ref, table_ref, qkv_ref, mixed_ref, prob_ref, out_ref):
    seq = x_ref.shape[0]
    tile = 128
    low = lax.broadcasted_iota(jnp.int32, (tile, LANES), 1) < HEAD_DIM
    for part in range(3):
        qkv_ref[part] = dot(x_ref[...], w_ref[part, 0, 0], NT).astype(BF)
    for start in range(0, seq, tile):
        rows = pl.ds(start, tile)
        query = qkv_ref[0, rows, :]
        mixed = []
        for head in range(2):
            part = jnp.where(low if head == 0 else ~low, query, jnp.zeros_like(query))
            scores = dot(part, qkv_ref[1], NT) * 0.125 + lookup(
                table_ref[0, head : head + 1, :], bucket_ref[rows, :]
            )
            scores = jnp.exp(scores - jnp.max(scores, axis=-1, keepdims=True))
            weights = (scores / jnp.sum(scores, axis=-1, keepdims=True)).astype(BF)
            prob_ref[head, rows, :] = weights
            mixed.append(dot(weights, qkv_ref[2]))
        mixed_ref[rows, :] = jnp.where(low, mixed[0], mixed[1]).astype(BF)
    out = dot(mixed_ref[...], w_ref[3, 0, 0])

    @pl.when(pl.program_id(0) == 0)
    def _():
        out_ref[...] = out

    @pl.when(pl.program_id(0) > 0)
    def _():
        out_ref[...] += out


def attend(x, weights, buckets, table, after):
    seq, width = x.shape
    _, pairs, groups, _, _ = weights.shape
    steps = pairs * groups
    full = pl.BlockSpec((seq, width), lambda i: (0, 0))
    col = pl.BlockSpec((seq, LANES), lambda i: (0, i))
    return launch(
        attend_kernel,
        (x, weights, buckets, table),
        after,
        grid=(steps,),
        in_specs=[
            full,
            pl.BlockSpec((4, 1, 1, LANES, width), lambda i: (0, i % pairs, i // pairs, 0, 0)),
            pl.BlockSpec((seq, seq), lambda i: (0, 0)),
            pl.BlockSpec((1, 2, LANES), lambda i: (i, 0, 0)),
        ],
        out_specs=[
            pl.BlockSpec((3, seq, LANES), lambda i: (0, 0, i)),
            col,
            pl.BlockSpec((2, seq, seq), lambda i: (i, 0, 0)),
            full,
        ],
        out_shape=[
            jax.ShapeDtypeStruct((3, seq, steps * LANES), BF),
            jax.ShapeDtypeStruct((seq, steps * LANES), BF),
            jax.ShapeDtypeStruct((2 * steps, seq, seq), BF),
            jax.ShapeDtypeStruct((seq, width), F32),
        ],
        name="attend",
        flops=steps * seq * LANES * 2 * (4 * width + 4 * seq),
    )


def attend_back_kernel(
    x_ref, grad_ref, w_ref, qkv_ref, mixed_ref, prob_ref, weight_ref, score_ref, normed_ref, part_ref
):
    seq = x_ref.shape[0]
    tile = 128
    low = lax.broadcasted_iota(jnp.int32, (tile, LANES), 1) < HEAD_DIM
    mixed_grad = dot(grad_ref[...], w_ref[3, 0, 0], NT).astype(BF)
    part_ref[...] = mixed_grad
    queries = []
    for start in range(0, seq, tile):
        rows = pl.ds(start, tile)
        grad = part_ref[rows, :]
        back = []
        for head in range(2):
            part = jnp.where(low if head == 0 else ~low, grad, jnp.zeros_like(grad))
            weights = prob_ref[head, rows, :].astype(F32)
            weight_grad = dot(part, qkv_ref[2], NT)
            score = weights * (
                weight_grad - jnp.sum(weights * weight_grad, axis=-1, keepdims=True)
            )
            score = score.astype(BF)
            score_ref[head, rows, :] = score
            back.append(dot(score, qkv_ref[1]))
        queries.append((jnp.where(low, back[0], back[1]) * 0.125).astype(BF))
    wide = lax.broadcasted_iota(jnp.int32, (seq, LANES), 1) < HEAD_DIM
    keys = [dot(score_ref[head], qkv_ref[0], TN) for head in range(2)]
    vals = [dot(prob_ref[head], mixed_grad, TN) for head in range(2)]
    back = jnp.concatenate(
        [
            jnp.concatenate(queries, 0),
            (jnp.where(wide, keys[0], keys[1]) * 0.125).astype(BF),
            jnp.where(wide, vals[0], vals[1]).astype(BF),
        ],
        1,
    )
    weight_ref[:3, 0, 0] = dot(back, x_ref[...], TN).reshape(3, LANES, -1).astype(BF)
    weight_ref[3, 0, 0] = dot(mixed_ref[...], grad_ref[...], TN).astype(BF)
    normed = dot(back, w_ref[:3, 0, 0].reshape(3 * LANES, -1))

    @pl.when(pl.program_id(0) == 0)
    def _():
        normed_ref[...] = normed

    @pl.when(pl.program_id(0) > 0)
    def _():
        normed_ref[...] += normed


def attend_back(x, grad, weights, qkv, mixed, probs, after):
    seq, width = x.shape
    _, pairs, groups, _, _ = weights.shape
    steps = pairs * groups
    full = pl.BlockSpec((seq, width), lambda i: (0, 0))
    col = pl.BlockSpec((seq, LANES), lambda i: (0, i))
    strip = pl.BlockSpec((4, 1, 1, LANES, width), lambda i: (0, i % pairs, i // pairs, 0, 0))
    square = pl.BlockSpec((2, seq, seq), lambda i: (i, 0, 0))
    return launch(
        attend_back_kernel,
        (x, grad, weights, qkv, mixed, probs),
        after,
        grid=(steps,),
        in_specs=[full, full, strip, pl.BlockSpec((3, seq, LANES), lambda i: (0, 0, i)), col, square],
        out_specs=[strip, square, full],
        out_shape=[
            jax.ShapeDtypeStruct((4, pairs, groups, LANES, width), BF),
            jax.ShapeDtypeStruct(probs.shape, BF),
            jax.ShapeDtypeStruct((seq, width), F32),
        ],
        scratch=[pltpu.VMEM((seq, LANES), BF)],
        name="attend_back",
        flops=steps * seq * LANES * 2 * (8 * width + 8 * seq),
    )


def table_kernel(*refs):
    *score_refs, bucket_ref, out_ref = refs
    marks = bucket_ref[...]
    tile, seq = marks.shape
    count = out_ref.shape[1] // tile
    ids = lax.broadcasted_iota(jnp.int32, (tile, count, seq), 1)
    onehot = (jnp.broadcast_to(marks[:, None, :], ids.shape) == ids).astype(F32)
    onehot = onehot.astype(BF).reshape(tile * count, seq)
    block = jnp.concatenate([ref[...].reshape(-1, seq) for ref in score_refs], 0)
    sums = dot(block, onehot, NT)

    @pl.when(pl.program_id(0) == 0)
    def _():
        out_ref[...] = sums

    @pl.when(pl.program_id(0) > 0)
    def _():
        out_ref[...] += sums


def table_back(scores, buckets, count, after):
    heads = sum(part.shape[0] for part in scores)
    seq = buckets.shape[0]
    tile = 16
    sums = launch(
        table_kernel,
        (*scores, buckets),
        after,
        grid=(seq // tile,),
        in_specs=[pl.BlockSpec((part.shape[0], tile, seq), lambda i: (0, i, 0)) for part in scores]
        + [pl.BlockSpec((tile, seq), lambda i: (i, 0))],
        out_specs=pl.BlockSpec((heads * tile, tile * count), lambda i: (0, 0)),
        out_shape=jax.ShapeDtypeStruct((heads * tile, tile * count), F32),
        name="table_back",
        flops=heads * tile * seq * seq * count * 2 * 4,
    )
    sums = sums.reshape(heads, tile, tile, count)
    same = jnp.eye(tile, dtype=F32)[None, :, :, None]
    return jnp.sum(sums * same, axis=(1, 2)).T


def assemble(place, halves, after):
    sources, groups, strip, _ = halves[0].shape
    width = sum(half.shape[3] for half in halves)
    held = [value for value in after if value is not None]

    def kernel(place_ref, *refs):
        refs[-1][0] = jnp.concatenate([ref[0] for ref in refs[: len(halves)]], -1)

    return pl.pallas_call(
        kernel,
        grid_spec=pltpu.PrefetchScalarGridSpec(
            num_scalar_prefetch=1,
            grid=(sources,),
            in_specs=[
                pl.BlockSpec((1, groups, strip, half.shape[3]), lambda i, at, side=side: (at[side, i], 0, 0, 0))
                for side, half in enumerate(halves)
            ]
            + [pl.BlockSpec(memory_space=pl.ANY)] * len(held),
            out_specs=pl.BlockSpec((1, groups, strip, width), lambda i, at: (i, 0, 0, 0)),
        ),
        out_shape=jax.ShapeDtypeStruct((sources, groups, strip, width), BF),
        cost_estimate=pl.CostEstimate(flops=0, bytes_accessed=4 * sources * groups * strip * width, transcendentals=0),
        name="assemble",
    )(place, *halves, *held)


def split_kernel(in_ref, *out_refs):
    cols = in_ref.shape[0] // 4
    for part, ref in enumerate(out_refs):
        rows = in_ref[part * cols : (part + 1) * cols, :].astype(F32)
        ref[...] = rows if part == 3 else rows.T


def split(value, after):
    rows, width = value.shape
    cols = rows // 4
    tile = min(width, 256)
    wide = pl.BlockSpec((tile, cols), lambda i: (i, 0))
    return launch(
        split_kernel,
        (value,),
        after,
        grid=(width // tile,),
        in_specs=[pl.BlockSpec((rows, tile), lambda i: (0, i))],
        out_specs=[wide, wide, wide, pl.BlockSpec((cols, tile), lambda i: (0, i))],
        out_shape=[jax.ShapeDtypeStruct((width, cols), F32)] * 3 + [jax.ShapeDtypeStruct((cols, width), F32)],
        name="split",
        flops=value.size,
    )


def copy_kernel(from_ref, to_ref):
    to_ref[...] = from_ref[...]


def hold(value, after):
    full = pl.BlockSpec(value.shape, lambda i: (0,) * value.ndim)
    return launch(
        copy_kernel,
        (value,),
        after,
        grid=(1,),
        in_specs=[full],
        out_specs=full,
        out_shape=jax.ShapeDtypeStruct(value.shape, value.dtype),
        name="hold",
        flops=0,
    )


def stack(place, parts, after):
    shape = parts[0].shape
    held = [value for value in after if value is not None]
    count = len(parts)

    def kernel(place_ref, *refs):
        for i in range(count):

            @pl.when(pl.program_id(0) == i)
            def _():
                refs[-1][...] = refs[i][...]

    full = pl.BlockSpec(shape, lambda s, at: (0,) * len(shape))
    return pl.pallas_call(
        kernel,
        grid_spec=pltpu.PrefetchScalarGridSpec(
            num_scalar_prefetch=1,
            grid=(count,),
            in_specs=[full] * count + [pl.BlockSpec(memory_space=pl.ANY)] * len(held),
            out_specs=pl.BlockSpec(shape, lambda s, at: (at[s],) + (0,) * (len(shape) - 1)),
        ),
        out_shape=jax.ShapeDtypeStruct((count * shape[0],) + shape[1:], BF),
        compiler_params=pltpu.CompilerParams(vmem_limit_bytes=58 * MIB),
        name="stack",
    )(place, *parts, *held)


def sum_kernel(*refs):
    *parts, out_ref = refs
    total = parts[0][...].astype(F32)
    for ref in parts[1:]:
        total += ref[...].astype(F32)
    out_ref[...] = total.astype(out_ref.dtype)


def add(*operands):
    *parts, after = operands
    shape = parts[0].shape
    if parts[0].ndim > 2:
        block = pl.BlockSpec((1,) + shape[1:], lambda i: (i,) + (0,) * (len(shape) - 1))
    else:
        block = pl.BlockSpec(shape, lambda i: (0, 0))
    return launch(
        sum_kernel,
        parts,
        after,
        grid=(shape[0] if len(shape) > 2 else 1,),
        in_specs=[block] * len(parts),
        out_specs=block,
        out_shape=jax.ShapeDtypeStruct(shape, parts[0].dtype),
        name="add",
        flops=parts[0].size,
    )


def dispatch_kernel(id_ref, x_ref, out_ref):
    count = out_ref.shape[0]
    slot = lax.broadcasted_iota(jnp.int32, (count, x_ref.shape[0]), 0) + pl.program_id(0) * count
    onehot = (slot == id_ref[0:1, :]) | (slot == id_ref[1:2, :])
    out_ref[...] = dot(onehot.astype(F32).astype(BF), x_ref[...]).astype(BF)


def to_slots(ids, value, slots, after):
    rows, width = value.shape
    steps = 4
    return launch(
        dispatch_kernel,
        (ids, value),
        after,
        grid=(steps,),
        in_specs=[
            pl.BlockSpec((TOP, rows), lambda i: (0, 0)),
            pl.BlockSpec((rows, width), lambda i: (0, 0)),
        ],
        out_specs=pl.BlockSpec((slots // steps, width), lambda i: (i, 0)),
        out_shape=jax.ShapeDtypeStruct((slots, width), BF),
        name="to_slots",
        flops=slots * rows * width * 2,
    )


def to_many_slots(place, ids, values, here, after):
    chunks = place.shape[0]
    _, rows, width = values.shape
    count = here[0] * here[1]
    held = [value for value in after if value is not None]
    steps = 2
    part = here[0] // steps

    def kernel(place_ref, id_ref, x_ref, *refs):
        out_ref = refs[-1]
        total = part * here[1]
        slot = lax.broadcasted_iota(jnp.int32, (total, rows), 0) + pl.program_id(1) * total
        onehot = (slot == id_ref[0, 0:1, :]) | (slot == id_ref[0, 1:2, :])
        out = dot(onehot.astype(F32).astype(BF), x_ref[0])
        out_ref[...] = out.reshape(out_ref.shape).astype(BF)

    return pl.pallas_call(
        kernel,
        grid_spec=pltpu.PrefetchScalarGridSpec(
            num_scalar_prefetch=1,
            grid=(chunks, steps),
            in_specs=[
                pl.BlockSpec((1, TOP, rows), lambda c, j, at: (c, 0, 0)),
                pl.BlockSpec((1, rows, width), lambda c, j, at: (at[c], 0, 0)),
            ]
            + [pl.BlockSpec(memory_space=pl.ANY)] * len(held),
            out_specs=pl.BlockSpec((part, 1, here[1], width), lambda c, j, at: (j, c, 0, 0)),
        ),
        out_shape=jax.ShapeDtypeStruct((here[0], chunks, here[1], width), BF),
        compiler_params=pltpu.CompilerParams(vmem_limit_bytes=58 * MIB),
        cost_estimate=pl.CostEstimate(
            flops=2 * chunks * count * rows * width, bytes_accessed=4 * chunks * count * width, transcendentals=0
        ),
        name="to_many_slots",
    )(place, ids, values, *held)


def collect_kernel(id_ref, slot_ref, *refs):
    *more, out_ref = refs
    rows = out_ref.shape[0]
    slot = lax.broadcasted_iota(jnp.int32, (rows, slot_ref.shape[0]), 1)
    onehot = (slot == id_ref[:, 0:1]) | (slot == id_ref[:, 1:2])
    total = dot(onehot.astype(F32).astype(BF), slot_ref[...])
    for ref in more:
        total += ref[...].astype(F32)
    out_ref[...] = total.astype(out_ref.dtype)


def to_tokens(ids, slots, more, kind, after):
    rows = ids.shape[0]
    count, width = slots.shape
    steps = 2
    block = pl.BlockSpec((rows // steps, width), lambda i: (i, 0))
    return launch(
        collect_kernel,
        (ids, slots, *more),
        after,
        grid=(steps,),
        in_specs=[
            pl.BlockSpec((rows // steps, TOP), lambda i: (i, 0)),
            pl.BlockSpec((count, width), lambda i: (0, 0)),
        ]
        + [block] * len(more),
        out_specs=block,
        out_shape=jax.ShapeDtypeStruct((rows, width), kind),
        name="to_tokens",
        flops=count * rows * width * 2,
    )


def flat(ref):
    block = ref[...]
    return block.astype(F32).reshape(-1, block.shape[-1]).astype(BF)


def expert_kernel(
    base_ref,
    x_ref,
    g_ref,
    other_ref,
    gate_ref,
    up_ref,
    down_ref,
    router_ref,
    out_ref,
    back_ref,
    hidden_ref,
    gate_back_ref,
    up_back_ref,
    route_ref,
):
    expert = pl.program_id(0)
    x = flat(x_ref)
    g = flat(g_ref)
    lanes = lax.broadcasted_iota(jnp.int32, (x.shape[0], LANES), 1)
    sign = (lanes == base_ref[0] + expert).astype(F32) - (lanes == other_ref[0]).astype(F32)
    logits = dot(x, router_ref[...])
    apart = jnp.sum(sign * (logits[:, :LANES] + logits[:, LANES:]), axis=-1, keepdims=True)
    weight = 1.0 / (1.0 + jnp.exp(-apart))
    gate = dot(x, gate_ref[0], NT)
    up = dot(x, up_ref[0], NT)
    grad = dot(g, down_ref[0], NT)
    scale = 0.7978845608028654
    square = gate * gate
    bent = jnp.tanh(scale * gate * (1.0 + 0.044715 * square))
    half = 0.5 + 0.5 * bent
    act = gate * half
    slope = half + 0.5 * gate * (1.0 - bent * bent) * (scale + 3 * 0.044715 * scale * square)
    hidden = act * up
    mark = weight * (1.0 - weight) * jnp.sum(hidden * grad, axis=-1, keepdims=True)
    mark = (mark * sign).astype(BF)
    grad = grad * weight
    up_back = (grad * act).astype(BF)
    gate_back = (grad * up * slope).astype(BF)
    hidden_ref[0] = (hidden * weight).astype(BF)
    gate_back_ref[0] = gate_back
    up_back_ref[0] = up_back
    out = dot(hidden.astype(BF), down_ref[0]) * weight
    out_ref[...] = out.reshape(out_ref.shape).astype(BF)
    back = dot(gate_back, gate_ref[0]) + dot(up_back, up_ref[0])
    back += dot(mark, router_ref[:, :LANES], NT)
    back_ref[...] = back.reshape(back_ref.shape).astype(BF)
    part = dot(mark, x, TN)

    @pl.when(expert == 0)
    def _():
        route_ref[...] = jnp.zeros_like(route_ref)

    route_ref[...] += part


def chunk_spec(array, chunk):
    sources, _, _, slots, width = array.shape
    return pl.BlockSpec((sources, 1, 1, slots, width), lambda e: (0, chunk, e, 0, 0))


def expert_chunk(base, x_at, g_at, other, gate_w, up_w, down_w, router_pair, after):
    (x, x_chunk), (g, g_chunk) = x_at, g_at
    sources, _, here, slots, width = x.shape
    hidden = down_w.shape[1]
    count = sources * slots
    rows = pl.BlockSpec((sources, 1, slots, width), lambda e: (0, e, 0, 0))
    middle = pl.BlockSpec((1, count, hidden), lambda e: (e, 0, 0))
    weights = pl.BlockSpec((1, hidden, width), lambda e: (e, 0, 0))
    return launch(
        expert_kernel,
        (base, x, g, other, gate_w, up_w, down_w, router_pair),
        after,
        grid=(here,),
        in_specs=[
            pl.BlockSpec(memory_space=pltpu.SMEM),
            chunk_spec(x, x_chunk),
            chunk_spec(g, g_chunk),
            pl.BlockSpec((1, count, 1), lambda e: (e, 0, 0)),
            weights,
            weights,
            weights,
            pl.BlockSpec((width, 2 * LANES), lambda e: (0, 0)),
        ],
        out_specs=[rows, rows, middle, middle, middle, pl.BlockSpec((LANES, width), lambda e: (0, 0))],
        out_shape=[jax.ShapeDtypeStruct((sources, here, slots, width), BF)] * 2
        + [jax.ShapeDtypeStruct((here, count, hidden), BF)] * 3
        + [jax.ShapeDtypeStruct((LANES, width), F32)],
        name="experts",
        flops=12 * here * count * width * hidden * 2,
    )


def weight_kernel(*refs, chunks):
    xs, gs, hidden, gates, ups = (refs[i * chunks : (i + 1) * chunks] for i in range(5))
    gate_ref, up_ref, down_ref = refs[5 * chunks :]
    x = jnp.concatenate([flat(ref) for ref in xs], 0)
    gate_ref[0] = dot(jnp.concatenate([ref[0] for ref in gates], 0), x, TN)
    up_ref[0] = dot(jnp.concatenate([ref[0] for ref in ups], 0), x, TN)
    g = jnp.concatenate([flat(ref) for ref in gs], 0)
    down_ref[0] = dot(jnp.concatenate([ref[0] for ref in hidden], 0), g, TN)


def weight_grads(xs, gs, hidden, gates, ups, after):
    sources, _, here, slots, width = xs[0][0].shape
    depth = hidden[0].shape[2]
    middle = pl.BlockSpec((1, sources * slots, depth), lambda e: (e, 0, 0))
    chunks = len(xs)
    return launch(
        functools.partial(weight_kernel, chunks=chunks),
        (*[v for v, _ in xs], *[v for v, _ in gs], *hidden, *gates, *ups),
        after,
        grid=(here,),
        in_specs=[chunk_spec(*v) for v in (*xs, *gs)] + [middle] * (3 * chunks),
        out_specs=[pl.BlockSpec((1, depth, width), lambda e: (e, 0, 0))] * 3,
        out_shape=[jax.ShapeDtypeStruct((here, depth, width), F32)] * 3,
        name="expert_weight_grads",
        flops=4 * here * chunks * sources * slots * width * depth * 2,
    )


def body(
    n_expert,
    n_tensor,
    inputs,
    gain_one,
    w_query,
    w_key,
    w_value,
    w_out,
    rel_table,
    gain_two,
    router,
    w_gate,
    w_up,
    w_down,
    routes,
    buckets,
    grad_out,
):
    rows, width = inputs.shape
    experts = router.shape[1]
    here = w_gate.shape[0]
    tokens = routes.shape[0]
    cap = (5 * rows * TOP + 4 * experts - 1) // (4 * experts)
    slots = experts * cap
    seq = buckets.shape[0]
    share = seq // rows
    count = rel_table.shape[0]
    head_cols = w_query.shape[1]
    at_expert = lax.axis_index("expert")
    at_tensor = lax.axis_index("tensor")
    steps = range(n_tensor)
    far = range(2, n_tensor)
    last = [None]

    def swap(value, step):
        return lax.ppermute(value, "tensor", [(i, i ^ step) for i in range(n_tensor)])

    def exchange(value):
        return lax.all_to_all(value, "expert", split_axis=0, concat_axis=0, tiled=True)

    def ordered(run, *operands, after=()):
        before = last[0] if isinstance(last[0], tuple) else (last[0],)
        result = run(*operands, (*before, *after))
        last[0] = result[0] if isinstance(result, (list, tuple)) else result
        return result

    labels = jnp.arange(experts, dtype=jnp.int32)
    grouped = routes.T.reshape(TOP, n_expert * n_tensor, rows)
    marks = (grouped[:, :, None, :] == labels[:, None]).astype(BF)
    order = jnp.arange(rows, dtype=jnp.int32)
    earlier = (order[:, None] < order[None, :]).astype(BF)
    ahead = jnp.einsum("kges,st->kget", marks, earlier, preferred_element_type=F32)
    first_count = jnp.sum(marks[0].astype(F32), axis=-1, keepdims=True)
    ahead = ahead + jnp.stack([jnp.zeros_like(first_count), first_count])
    places = jnp.sum(ahead * marks.astype(F32), axis=2).astype(jnp.int32)
    slot_ids = jnp.where(places < cap, grouped * cap + places, -1)
    slot_ids = slot_ids.reshape(TOP, n_expert, n_tensor, rows)
    choices = grouped.reshape(TOP, n_expert, n_tensor, rows)

    def relative(value, axis):
        return jnp.stack([lax.dynamic_index_in_dim(value, at_tensor ^ i, axis, keepdims=False) for i in steps])

    own_ids = relative(lax.dynamic_index_in_dim(slot_ids, at_expert, 1, keepdims=False), 1)
    id_rows = [own_ids[i] for i in steps]
    id_cols = jnp.swapaxes(own_ids, 1, 2)
    local = slot_ids - at_expert * (here * cap)
    slot_here = jnp.arange(here * cap, dtype=jnp.int32)[:, None]
    partner = jnp.sum(
        jnp.where(local[0][:, :, None, :] == slot_here, choices[1][:, :, None, :], 0)
        + jnp.where(local[1][:, :, None, :] == slot_here, choices[0][:, :, None, :], 0),
        axis=-1,
    ).reshape(n_expert, n_tensor, here, cap)
    partners = jnp.swapaxes(relative(partner, 1), 1, 2).reshape(n_tensor, here, n_expert * cap, 1)

    def send(step, value, after=()):
        buffer = ordered(to_slots, id_rows[step], value, slots, after=after)
        return exchange(buffer.reshape(n_expert, here, cap, width))

    def home(step, value, more=(), kind=BF, after=()):
        return ordered(to_tokens, id_cols[step], value.reshape(slots, width), more, kind, after=after)

    def gather(value):
        whole = lax.all_gather(value, "tensor", axis=0, tiled=True).reshape(n_tensor, rows, width)
        return [lax.dynamic_index_in_dim(whole, at_tensor ^ i, 0, keepdims=False) for i in steps]

    def everywhere(values):
        total = jnp.concatenate([value.reshape(-1) for value in values])
        for axis, size in (("expert", n_expert), ("tensor", n_tensor)):
            for bit in range(size.bit_length() - 1):
                total = total + lax.ppermute(total, axis, [(i, i ^ (1 << bit)) for i in range(size)])
        totals = []
        for value in values:
            totals.append(total[: value.size].reshape(value.shape))
            total = total[value.size :]
        return totals

    def whole_seq(value):
        if share == 1:
            return value
        groups = [[i * share + j for j in range(share)] for i in range(n_tensor // share)]
        return lax.all_gather(value, "tensor", axis=0, tiled=True, axis_index_groups=groups)

    def own_rows(value):
        if share == 1:
            return value
        return lax.dynamic_slice_in_dim(value, (at_tensor % share) * rows, rows, 0)

    packed = jnp.concatenate([w_query.T, w_key.T, w_value.T, w_out], 0)
    strip = 4 * head_cols // n_expert
    blocks = 4 * head_cols // LANES
    pairs = blocks // 4
    own_w = packed.reshape(4, pairs, 1, LANES, width)
    packed = ordered(hold, lax.dynamic_slice_in_dim(packed, at_expert * strip, strip, 0))
    strips = jnp.stack([swap(packed, i) for i in steps[1:]])
    table_own = jnp.pad(rel_table.T, ((0, 0), (0, LANES - count)))
    table_all = jnp.stack([table_own] + [swap(table_own, i) for i in steps[1:]])
    table_all = table_all.reshape(n_tensor * pairs, 2, LANES)

    inputs_f = inputs.astype(F32)
    normed_one = rms_scale(inputs_f, gain_one).astype(BF)
    attn_in = whole_seq(normed_one)
    grad_low = ordered(hold, grad_out, after=(strips, table_all))
    grad_all = lax.all_gather(grad_low, "tensor", axis=0, tiled=True).reshape(n_tensor, rows, width)
    own_part = ordered(attend, attn_in, own_w, buckets, table_all[:pairs])

    bits = [1 << i for i in range(1, n_expert.bit_length() - 1)]
    sources = jnp.arange(n_expert, dtype=jnp.int32) ^ at_expert
    halves, places, came = [], [], []
    for half in range(2):
        held, order = strips[None, :, :, half * width // 2 : (half + 1) * width // 2], [0]
        for bit in (bits if half == 0 else bits[::-1]) + [1]:
            came.append(held)
            held = jnp.concatenate([held, lax.ppermute(held, "expert", [(i, i ^ bit) for i in range(n_expert)])], 0)
            order = order + [i ^ bit for i in order]
        halves.append(held)
        where = jnp.asarray([order.index(i) for i in range(n_expert)], jnp.int32)
        places.append(jnp.sum(jnp.where(sources[:, None] == jnp.arange(n_expert), where, 0), 1))
    places = jnp.stack(places).astype(jnp.int32)

    grad_own = send(0, grad_out, (came[len(bits)], came[-1]))
    attn_w = ordered(assemble, places, halves)
    others = jnp.arange(1, n_tensor, dtype=jnp.int32) ^ at_tensor
    grad_rest = exchange(
        ordered(to_many_slots, others, own_ids[1:], grad_all, (n_expert, here * cap), after=(grad_own,))
    )
    grad_slots = {0: (grad_own, 0)} | {i: (grad_rest, i - 1) for i in steps[1:]}
    attn_w = attn_w.reshape(blocks, n_expert // blocks, n_tensor - 1, strip, width)
    attn_w = jnp.swapaxes(attn_w, 1, 2).reshape(4, pairs, n_tensor - 1, LANES, width)
    rest_part = ordered(attend, attn_in, attn_w, buckets, table_all[pairs:])
    resid = inputs_f + own_rows(own_part[3] + rest_part[3])
    normed_two = rms_scale(resid, gain_two)
    normed_low = normed_two.astype(BF)

    token_far = gather(normed_low)
    token_slots = {0: send(0, normed_low, (grad_rest,))}

    counts = jnp.sum((routes.T[:, None, :] == labels[:, None]).astype(F32), axis=(0, 2))
    route_share = counts / (tokens * TOP)

    def losses(normed, router_w):
        logits = jnp.dot(normed, router_w, precision=highest)
        router_probs = jax.nn.softmax(logits, axis=-1)
        log_totals = jax.nn.logsumexp(logits, axis=-1)
        balance = experts * jnp.sum(route_share * jnp.sum(router_probs, axis=0)) / tokens
        return balance, jnp.sum(log_totals * log_totals) / tokens

    (balance_part, zloss_part), losses_back = jax.vjp(losses, normed_two, router)
    normed_grad, router_grad = losses_back(
        (jnp.asarray(balance_weight, F32), jnp.asarray(zloss_weight, F32))
    )

    router_high = router.astype(BF)
    router_low = (router - router_high.astype(F32)).astype(BF)
    fill = ((0, 0), (0, LANES - experts))
    router_pair = jnp.concatenate([jnp.pad(router_high, fill), jnp.pad(router_low, fill)], 1)
    base = jnp.full((1,), at_expert * here, jnp.int32)
    gate_w = jnp.swapaxes(w_gate, 1, 2)
    up_w = jnp.swapaxes(w_up, 1, 2)

    def rows_in(value):
        value, chunk = value
        if cap % 8 == 0:
            return value.reshape(n_expert, -1, here, cap, width), chunk
        value = value.reshape(n_expert, -1, here, cap, width)[:, chunk]
        return jnp.swapaxes(value, 0, 1).reshape(1, 1, here, n_expert * cap, width), 0

    def rows_out(value):
        if cap % 8 == 0:
            return value
        return jnp.swapaxes(value.reshape(here, n_expert, cap, width), 0, 1)

    xs, gs, done = {}, {}, {}

    def work(step):
        xs[step], gs[step] = rows_in((token_slots[step], 0)), rows_in(grad_slots[step])
        done[step] = ordered(
            expert_chunk, base, xs[step], gs[step], partners[step], gate_w, up_w, w_down, router_pair
        )

    token_slots[1] = send(1, token_far[1])
    work(0)
    for i in far:
        token_slots[i] = send(i, token_far[i])
        work(i - 1)
    work(n_tensor - 1)
    backs = {i: rows_out(done[i][1]) for i in steps}
    outs = {i: rows_out(done[i][0]) for i in steps}
    moe_far, near = [], None
    for i in far:
        moe_far.append(swap(home(i, exchange(backs[i]), after=moe_far[-1:]), i))
        if i == far[0]:
            near = exchange(ordered(add, backs[0], swap(backs[1], 1)))
    gate_grad, up_grad, down_grad = ordered(
        weight_grads,
        *[[v[i] for i in steps] for v in (xs, gs)],
        *[[done[i][j] for i in steps] for j in (2, 3, 4)],
    )
    moe_grad = home(0, near, moe_far, F32)
    router_grad = router_grad + sum(done[i][5] for i in steps)[:experts].T

    grad_f = grad_out.astype(F32)
    resid_norm_grad, gain_two_grad = jax.vjp(rms_scale, resid, gain_two)[1](normed_grad + moe_grad)
    resid_grad = grad_f + resid_norm_grad
    attn_grad = whole_seq(resid_grad.astype(BF))
    out_all = ordered(stack, jnp.arange(n_tensor, dtype=jnp.int32) ^ at_tensor, [outs[i] for i in steps])
    rest_back = ordered(attend_back, attn_in, attn_grad, attn_w, *rest_part[:3])
    own_back = ordered(attend_back, attn_in, attn_grad, own_w, *own_part[:3])
    out_sum = lax.psum_scatter(out_all, "tensor", scatter_dimension=0, tiled=True)
    out_sum = exchange(out_sum.reshape(n_expert, here, cap, width))
    normed_one_grad = own_back[2] + rest_back[2]

    side = at_expert % 2

    def pair_sum(weight_parts):
        groups = weight_parts.shape[2]
        parts = weight_parts.reshape(blocks, groups, n_expert // blocks, strip, width)
        parts = jnp.swapaxes(parts, 1, 2).reshape(n_expert // 2, 2, groups, strip, width)
        kept = lax.dynamic_index_in_dim(parts, side, 1, keepdims=False)
        given = lax.dynamic_index_in_dim(parts, 1 - side, 1, keepdims=False)
        given = lax.ppermute(given, "expert", [(i, i ^ 1) for i in range(n_expert)])
        return (kept.astype(F32) + given.astype(F32)).astype(BF)

    def plane_sum(parts):
        parts = lax.all_to_all(
            parts,
            "expert",
            split_axis=0,
            concat_axis=0,
            tiled=True,
            axis_index_groups=[list(range(i, n_expert, 2)) for i in range(2)],
        )
        return jnp.sum(parts.astype(F32), axis=0).astype(BF)

    parts = [pair_sum(own_back[0]), pair_sum(rest_back[0])]
    parts = [plane_sum(part) for part in parts]
    parts = [part[i] for part in parts for i in range(part.shape[0])]
    table_grad = ordered(table_back, (own_back[1], rest_back[1]), buckets, count)
    input_norm_grad, gain_one_grad = jax.vjp(rms_scale, inputs_f, gain_one)[1](own_rows(normed_one_grad))
    input_grad = resid_grad + input_norm_grad

    table_grad = relative(table_grad.T.reshape(n_tensor, rel_table.shape[1], count), 0) / share
    small = [router_grad.T, gain_one_grad, gain_two_grad, table_grad, jnp.stack([balance_part, zloss_part])]
    router_total, gain_one_total, gain_two_total, table_total, loss_total = everywhere(small)
    strip_grad = ordered(add, parts[0], *[swap(parts[i], i) for i in steps[1:]], after=(gain_one_total,))
    if share > 1:
        strip_grad = (strip_grad.astype(F32) / share).astype(BF)
    output = home(0, out_sum, (resid,), BF)

    attn_w_grad = lax.all_gather(strip_grad, "expert", axis=0, tiled=True)
    query_grad, key_grad, value_grad, out_proj_grad = ordered(split, attn_w_grad)
    table_total = lax.dynamic_index_in_dim(table_total, at_tensor, 0, keepdims=False).T
    return (
        output,
        input_grad,
        gain_one_total,
        query_grad,
        key_grad,
        value_grad,
        out_proj_grad,
        table_total,
        gain_two_total,
        router_total.T,
        jnp.swapaxes(gate_grad, 1, 2),
        jnp.swapaxes(up_grad, 1, 2),
        down_grad,
        loss_total,
    )


def solution(mesh):
    return jax.shard_map(
        functools.partial(body, mesh.shape["expert"], mesh.shape["tensor"]),
        mesh=mesh,
        in_specs=(
            P(("expert", "tensor"), None),
            P(),
            P(None, "tensor"),
            P(None, "tensor"),
            P(None, "tensor"),
            P("tensor", None),
            P(None, "tensor"),
            P(),
            P(),
            P("expert", None, "tensor"),
            P("expert", None, "tensor"),
            P("expert", "tensor", None),
            P(),
            P(),
            P(("expert", "tensor"), None),
        ),
        out_specs=(
            P(("expert", "tensor"), None),
            P(("expert", "tensor"), None),
            P(),
            P(None, "tensor"),
            P(None, "tensor"),
            P(None, "tensor"),
            P("tensor", None),
            P(None, "tensor"),
            P(),
            P(),
            P("expert", None, "tensor"),
            P("expert", None, "tensor"),
            P("expert", "tensor", None),
            P(),
        ),
        check_vma=False,
    )
```

```python
import functools

import jax
import jax.numpy as jnp
from jax import lax
from jax.experimental import pallas as pl
from jax.experimental.pallas import tpu as pltpu
from jax.sharding import PartitionSpec as P

HEAD_DIM = 64
TOP = 2
LANES = 128
MIB = 2**20

epsilon = 1e-06
balance_weight = 0.01
zloss_weight = 0.001
highest = lax.Precision.HIGHEST

BF = jnp.bfloat16
F32 = jnp.float32
NN = (((1,), (0,)), ((), ()))
NT = (((1,), (1,)), ((), ()))
TN = (((0,), (0,)), ((), ()))


def dot(left, right, dims=NN):
    return lax.dot_general(left, right, dims, preferred_element_type=F32)


def rms_scale(rows_in, gain):
    inverse = lax.rsqrt(jnp.mean(rows_in * rows_in, axis=-1, keepdims=True) + epsilon)
    return rows_in * inverse * gain


def drop(kernel, at, count):
    def run(*refs):
        kernel(*refs[:at], *refs[at + count :])

    return run


def launch(kernel, operands, after, *, grid, in_specs, out_specs, out_shape, name, flops, scratch=(), moved=0):
    held = [value for value in after if value is not None]
    sizes = [jax.ShapeDtypeStruct(v.shape, v.dtype) for v in operands] + jax.tree.leaves(out_shape)
    moved = moved or sum(v.size * v.dtype.itemsize for v in sizes)
    return pl.pallas_call(
        drop(kernel, len(operands), len(held)),
        grid=grid,
        in_specs=list(in_specs) + [pl.BlockSpec(memory_space=pl.ANY)] * len(held),
        out_specs=out_specs,
        out_shape=out_shape,
        scratch_shapes=scratch,
        compiler_params=pltpu.CompilerParams(vmem_limit_bytes=58 * MIB),
        cost_estimate=pl.CostEstimate(flops=flops, bytes_accessed=moved, transcendentals=0),
        name=name,
    )(*operands, *held)


def lookup(row, index):
    table = jnp.broadcast_to(row, (index.shape[0], LANES))
    parts = [
        jnp.take_along_axis(table, index[:, at : at + LANES], axis=1)
        for at in range(0, index.shape[1], LANES)
    ]
    return jnp.concatenate(parts, axis=1)


def attend_kernel(x_ref, w_ref, bucket_ref, table_ref, qkv_ref, mixed_ref, prob_ref, out_ref):
    seq = x_ref.shape[0]
    tile = 128
    low = lax.broadcasted_iota(jnp.int32, (tile, LANES), 1) < HEAD_DIM
    for part in range(3):
        qkv_ref[part] = dot(x_ref[...], w_ref[part, 0, 0], NT).astype(BF)
    for start in range(0, seq, tile):
        rows = pl.ds(start, tile)
        query = qkv_ref[0, rows, :]
        mixed = []
        for head in range(2):
            part = jnp.where(low if head == 0 else ~low, query, jnp.zeros_like(query))
            scores = dot(part, qkv_ref[1], NT) * 0.125 + lookup(
                table_ref[0, head : head + 1, :], bucket_ref[rows, :]
            )
            scores = jnp.exp(scores - jnp.max(scores, axis=-1, keepdims=True))
            weights = (scores / jnp.sum(scores, axis=-1, keepdims=True)).astype(BF)
            prob_ref[head, rows, :] = weights
            mixed.append(dot(weights, qkv_ref[2]))
        mixed_ref[rows, :] = jnp.where(low, mixed[0], mixed[1]).astype(BF)
    out = dot(mixed_ref[...], w_ref[3, 0, 0])

    @pl.when(pl.program_id(0) == 0)
    def _():
        out_ref[...] = out

    @pl.when(pl.program_id(0) > 0)
    def _():
        out_ref[...] += out


def attend(x, weights, buckets, table, after):
    seq, width = x.shape
    _, pairs, groups, _, _ = weights.shape
    steps = pairs * groups
    full = pl.BlockSpec((seq, width), lambda i: (0, 0))
    col = pl.BlockSpec((seq, LANES), lambda i: (0, i))
    return launch(
        attend_kernel,
        (x, weights, buckets, table),
        after,
        grid=(steps,),
        in_specs=[
            full,
            pl.BlockSpec((4, 1, 1, LANES, width), lambda i: (0, i % pairs, i // pairs, 0, 0)),
            pl.BlockSpec((seq, seq), lambda i: (0, 0)),
            pl.BlockSpec((1, 2, LANES), lambda i: (i, 0, 0)),
        ],
        out_specs=[
            pl.BlockSpec((3, seq, LANES), lambda i: (0, 0, i)),
            col,
            pl.BlockSpec((2, seq, seq), lambda i: (i, 0, 0)),
            full,
        ],
        out_shape=[
            jax.ShapeDtypeStruct((3, seq, steps * LANES), BF),
            jax.ShapeDtypeStruct((seq, steps * LANES), BF),
            jax.ShapeDtypeStruct((2 * steps, seq, seq), BF),
            jax.ShapeDtypeStruct((seq, width), F32),
        ],
        name="attend",
        flops=steps * seq * LANES * 2 * (4 * width + 4 * seq),
    )


def attend_back_kernel(
    x_ref, grad_ref, w_ref, qkv_ref, mixed_ref, prob_ref, weight_ref, score_ref, normed_ref, part_ref
):
    seq = x_ref.shape[0]
    tile = 128
    low = lax.broadcasted_iota(jnp.int32, (tile, LANES), 1) < HEAD_DIM
    mixed_grad = dot(grad_ref[...], w_ref[3, 0, 0], NT).astype(BF)
    part_ref[...] = mixed_grad
    queries = []
    for start in range(0, seq, tile):
        rows = pl.ds(start, tile)
        grad = part_ref[rows, :]
        back = []
        for head in range(2):
            part = jnp.where(low if head == 0 else ~low, grad, jnp.zeros_like(grad))
            weights = prob_ref[head, rows, :].astype(F32)
            weight_grad = dot(part, qkv_ref[2], NT)
            score = weights * (
                weight_grad - jnp.sum(weights * weight_grad, axis=-1, keepdims=True)
            )
            score = score.astype(BF)
            score_ref[head, rows, :] = score
            back.append(dot(score, qkv_ref[1]))
        queries.append((jnp.where(low, back[0], back[1]) * 0.125).astype(BF))
    wide = lax.broadcasted_iota(jnp.int32, (seq, LANES), 1) < HEAD_DIM
    keys = [dot(score_ref[head], qkv_ref[0], TN) for head in range(2)]
    vals = [dot(prob_ref[head], mixed_grad, TN) for head in range(2)]
    back = jnp.concatenate(
        [
            jnp.concatenate(queries, 0),
            (jnp.where(wide, keys[0], keys[1]) * 0.125).astype(BF),
            jnp.where(wide, vals[0], vals[1]).astype(BF),
        ],
        1,
    )
    weight_ref[:3, 0, 0] = dot(back, x_ref[...], TN).reshape(3, LANES, -1).astype(BF)
    weight_ref[3, 0, 0] = dot(mixed_ref[...], grad_ref[...], TN).astype(BF)
    normed = dot(back, w_ref[:3, 0, 0].reshape(3 * LANES, -1))

    @pl.when(pl.program_id(0) == 0)
    def _():
        normed_ref[...] = normed

    @pl.when(pl.program_id(0) > 0)
    def _():
        normed_ref[...] += normed


def attend_back(x, grad, weights, qkv, mixed, probs, after):
    seq, width = x.shape
    _, pairs, groups, _, _ = weights.shape
    steps = pairs * groups
    full = pl.BlockSpec((seq, width), lambda i: (0, 0))
    col = pl.BlockSpec((seq, LANES), lambda i: (0, i))
    strip = pl.BlockSpec((4, 1, 1, LANES, width), lambda i: (0, i % pairs, i // pairs, 0, 0))
    square = pl.BlockSpec((2, seq, seq), lambda i: (i, 0, 0))
    return launch(
        attend_back_kernel,
        (x, grad, weights, qkv, mixed, probs),
        after,
        grid=(steps,),
        in_specs=[full, full, strip, pl.BlockSpec((3, seq, LANES), lambda i: (0, 0, i)), col, square],
        out_specs=[strip, square, full],
        out_shape=[
            jax.ShapeDtypeStruct((4, pairs, groups, LANES, width), BF),
            jax.ShapeDtypeStruct(probs.shape, BF),
            jax.ShapeDtypeStruct((seq, width), F32),
        ],
        scratch=[pltpu.VMEM((seq, LANES), BF)],
        name="attend_back",
        flops=steps * seq * LANES * 2 * (8 * width + 8 * seq),
    )


def table_kernel(*refs):
    *score_refs, bucket_ref, out_ref = refs
    marks = bucket_ref[...]
    tile, seq = marks.shape
    count = out_ref.shape[1] // tile
    ids = lax.broadcasted_iota(jnp.int32, (tile, count, seq), 1)
    onehot = (jnp.broadcast_to(marks[:, None, :], ids.shape) == ids).astype(F32)
    onehot = onehot.astype(BF).reshape(tile * count, seq)
    block = jnp.concatenate([ref[...].reshape(-1, seq) for ref in score_refs], 0)
    sums = dot(block, onehot, NT)

    @pl.when(pl.program_id(0) == 0)
    def _():
        out_ref[...] = sums

    @pl.when(pl.program_id(0) > 0)
    def _():
        out_ref[...] += sums


def table_back(scores, buckets, count, after):
    heads = sum(part.shape[0] for part in scores)
    seq = buckets.shape[0]
    tile = 16
    sums = launch(
        table_kernel,
        (*scores, buckets),
        after,
        grid=(seq // tile,),
        in_specs=[pl.BlockSpec((part.shape[0], tile, seq), lambda i: (0, i, 0)) for part in scores]
        + [pl.BlockSpec((tile, seq), lambda i: (i, 0))],
        out_specs=pl.BlockSpec((heads * tile, tile * count), lambda i: (0, 0)),
        out_shape=jax.ShapeDtypeStruct((heads * tile, tile * count), F32),
        name="table_back",
        flops=heads * tile * seq * seq * count * 2 * 4,
    )
    sums = sums.reshape(heads, tile, tile, count)
    same = jnp.eye(tile, dtype=F32)[None, :, :, None]
    return jnp.sum(sums * same, axis=(1, 2)).T


def assemble(place, halves, after):
    sources, groups, strip, _ = halves[0].shape
    width = sum(half.shape[3] for half in halves)
    held = [value for value in after if value is not None]

    def kernel(place_ref, *refs):
        refs[-1][0] = jnp.concatenate([ref[0] for ref in refs[: len(halves)]], -1)

    return pl.pallas_call(
        kernel,
        grid_spec=pltpu.PrefetchScalarGridSpec(
            num_scalar_prefetch=1,
            grid=(sources,),
            in_specs=[
                pl.BlockSpec((1, groups, strip, half.shape[3]), lambda i, at, side=side: (at[side, i], 0, 0, 0))
                for side, half in enumerate(halves)
            ]
            + [pl.BlockSpec(memory_space=pl.ANY)] * len(held),
            out_specs=pl.BlockSpec((1, groups, strip, width), lambda i, at: (i, 0, 0, 0)),
        ),
        out_shape=jax.ShapeDtypeStruct((sources, groups, strip, width), BF),
        cost_estimate=pl.CostEstimate(flops=0, bytes_accessed=4 * sources * groups * strip * width, transcendentals=0),
        name="assemble",
    )(place, *halves, *held)


def split_kernel(in_ref, *out_refs):
    cols = in_ref.shape[0] // 4
    for part, ref in enumerate(out_refs):
        rows = in_ref[part * cols : (part + 1) * cols, :].astype(F32)
        ref[...] = rows if part == 3 else rows.T


def split(value, after):
    rows, width = value.shape
    cols = rows // 4
    tile = min(width, 256)
    wide = pl.BlockSpec((tile, cols), lambda i: (i, 0))
    return launch(
        split_kernel,
        (value,),
        after,
        grid=(width // tile,),
        in_specs=[pl.BlockSpec((rows, tile), lambda i: (0, i))],
        out_specs=[wide, wide, wide, pl.BlockSpec((cols, tile), lambda i: (0, i))],
        out_shape=[jax.ShapeDtypeStruct((width, cols), F32)] * 3 + [jax.ShapeDtypeStruct((cols, width), F32)],
        name="split",
        flops=value.size,
    )


def copy_kernel(from_ref, to_ref):
    to_ref[...] = from_ref[...]


def hold(value, after):
    full = pl.BlockSpec(value.shape, lambda i: (0,) * value.ndim)
    return launch(
        copy_kernel,
        (value,),
        after,
        grid=(1,),
        in_specs=[full],
        out_specs=full,
        out_shape=jax.ShapeDtypeStruct(value.shape, value.dtype),
        name="hold",
        flops=0,
    )


def stack(place, parts, after):
    shape = parts[0].shape
    held = [value for value in after if value is not None]
    count = len(parts)

    def kernel(place_ref, *refs):
        for i in range(count):

            @pl.when(pl.program_id(0) == i)
            def _():
                refs[-1][...] = refs[i][...]

    full = pl.BlockSpec(shape, lambda s, at: (0,) * len(shape))
    return pl.pallas_call(
        kernel,
        grid_spec=pltpu.PrefetchScalarGridSpec(
            num_scalar_prefetch=1,
            grid=(count,),
            in_specs=[full] * count + [pl.BlockSpec(memory_space=pl.ANY)] * len(held),
            out_specs=pl.BlockSpec(shape, lambda s, at: (at[s],) + (0,) * (len(shape) - 1)),
        ),
        out_shape=jax.ShapeDtypeStruct((count * shape[0],) + shape[1:], BF),
        compiler_params=pltpu.CompilerParams(vmem_limit_bytes=58 * MIB),
        name="stack",
    )(place, *parts, *held)


def sum_kernel(*refs):
    *parts, out_ref = refs
    total = parts[0][...].astype(F32)
    for ref in parts[1:]:
        total += ref[...].astype(F32)
    out_ref[...] = total.astype(out_ref.dtype)


def add(*operands):
    *parts, after = operands
    shape = parts[0].shape
    if parts[0].ndim > 2:
        block = pl.BlockSpec((1,) + shape[1:], lambda i: (i,) + (0,) * (len(shape) - 1))
    else:
        block = pl.BlockSpec(shape, lambda i: (0, 0))
    return launch(
        sum_kernel,
        parts,
        after,
        grid=(shape[0] if len(shape) > 2 else 1,),
        in_specs=[block] * len(parts),
        out_specs=block,
        out_shape=jax.ShapeDtypeStruct(shape, parts[0].dtype),
        name="add",
        flops=parts[0].size,
    )


def dispatch_kernel(id_ref, x_ref, out_ref):
    count = out_ref.shape[0]
    slot = lax.broadcasted_iota(jnp.int32, (count, x_ref.shape[0]), 0) + pl.program_id(0) * count
    onehot = (slot == id_ref[0:1, :]) | (slot == id_ref[1:2, :])
    out_ref[...] = dot(onehot.astype(F32).astype(BF), x_ref[...]).astype(BF)


def to_slots(ids, value, slots, after):
    rows, width = value.shape
    steps = 2
    return launch(
        dispatch_kernel,
        (ids, value),
        after,
        grid=(steps,),
        in_specs=[
            pl.BlockSpec((TOP, rows), lambda i: (0, 0)),
            pl.BlockSpec((rows, width), lambda i: (0, 0)),
        ],
        out_specs=pl.BlockSpec((slots // steps, width), lambda i: (i, 0)),
        out_shape=jax.ShapeDtypeStruct((slots, width), BF),
        name="to_slots",
        flops=slots * rows * width * 2,
    )


def to_many_slots(place, ids, values, here, after):
    chunks = place.shape[0]
    _, rows, width = values.shape
    count = here[0] * here[1]
    held = [value for value in after if value is not None]
    steps = 2
    part = here[0] // steps

    def kernel(place_ref, id_ref, x_ref, *refs):
        out_ref = refs[-1]
        total = part * here[1]
        slot = lax.broadcasted_iota(jnp.int32, (total, rows), 0) + pl.program_id(1) * total
        onehot = (slot == id_ref[0, 0:1, :]) | (slot == id_ref[0, 1:2, :])
        out = dot(onehot.astype(F32).astype(BF), x_ref[0])
        out_ref[...] = out.reshape(out_ref.shape).astype(BF)

    return pl.pallas_call(
        kernel,
        grid_spec=pltpu.PrefetchScalarGridSpec(
            num_scalar_prefetch=1,
            grid=(chunks, steps),
            in_specs=[
                pl.BlockSpec((1, TOP, rows), lambda c, j, at: (c, 0, 0)),
                pl.BlockSpec((1, rows, width), lambda c, j, at: (at[c], 0, 0)),
            ]
            + [pl.BlockSpec(memory_space=pl.ANY)] * len(held),
            out_specs=pl.BlockSpec((part, 1, here[1], width), lambda c, j, at: (j, c, 0, 0)),
        ),
        out_shape=jax.ShapeDtypeStruct((here[0], chunks, here[1], width), BF),
        compiler_params=pltpu.CompilerParams(vmem_limit_bytes=58 * MIB),
        cost_estimate=pl.CostEstimate(
            flops=2 * chunks * count * rows * width, bytes_accessed=4 * chunks * count * width, transcendentals=0
        ),
        name="to_many_slots",
    )(place, ids, values, *held)


def collect_kernel(id_ref, slot_ref, *refs):
    *more, out_ref = refs
    rows = out_ref.shape[0]
    slot = lax.broadcasted_iota(jnp.int32, (rows, slot_ref.shape[0]), 1)
    onehot = (slot == id_ref[:, 0:1]) | (slot == id_ref[:, 1:2])
    total = dot(onehot.astype(F32).astype(BF), slot_ref[...])
    for ref in more:
        total += ref[...].astype(F32)
    out_ref[...] = total.astype(out_ref.dtype)


def to_tokens(ids, slots, more, kind, after):
    rows = ids.shape[0]
    count, width = slots.shape
    steps = 2
    block = pl.BlockSpec((rows // steps, width), lambda i: (i, 0))
    return launch(
        collect_kernel,
        (ids, slots, *more),
        after,
        grid=(steps,),
        in_specs=[
            pl.BlockSpec((rows // steps, TOP), lambda i: (i, 0)),
            pl.BlockSpec((count, width), lambda i: (0, 0)),
        ]
        + [block] * len(more),
        out_specs=block,
        out_shape=jax.ShapeDtypeStruct((rows, width), kind),
        name="to_tokens",
        flops=count * rows * width * 2,
    )


def flat(ref):
    block = ref[...]
    return block.astype(F32).reshape(-1, block.shape[-1]).astype(BF)


def expert_kernel(
    base_ref,
    x_ref,
    g_ref,
    other_ref,
    gate_ref,
    up_ref,
    down_ref,
    router_ref,
    out_ref,
    back_ref,
    hidden_ref,
    gate_back_ref,
    up_back_ref,
    route_ref,
):
    expert = pl.program_id(0)
    x = flat(x_ref)
    g = flat(g_ref)
    lanes = lax.broadcasted_iota(jnp.int32, (x.shape[0], LANES), 1)
    sign = (lanes == base_ref[0] + expert).astype(F32) - (lanes == other_ref[0]).astype(F32)
    logits = dot(x, router_ref[...])
    apart = jnp.sum(sign * (logits[:, :LANES] + logits[:, LANES:]), axis=-1, keepdims=True)
    weight = 1.0 / (1.0 + jnp.exp(-apart))
    gate = dot(x, gate_ref[0], NT)
    up = dot(x, up_ref[0], NT)
    grad = dot(g, down_ref[0], NT)
    scale = 0.7978845608028654
    square = gate * gate
    bent = jnp.tanh(scale * gate * (1.0 + 0.044715 * square))
    half = 0.5 + 0.5 * bent
    act = gate * half
    slope = half + 0.5 * gate * (1.0 - bent * bent) * (scale + 3 * 0.044715 * scale * square)
    hidden = act * up
    mark = weight * (1.0 - weight) * jnp.sum(hidden * grad, axis=-1, keepdims=True)
    mark = (mark * sign).astype(BF)
    grad = grad * weight
    up_back = (grad * act).astype(BF)
    gate_back = (grad * up * slope).astype(BF)
    hidden_ref[0] = (hidden * weight).astype(BF)
    gate_back_ref[0] = gate_back
    up_back_ref[0] = up_back
    out = dot(hidden.astype(BF), down_ref[0]) * weight
    out_ref[...] = out.reshape(out_ref.shape).astype(BF)
    back = dot(gate_back, gate_ref[0]) + dot(up_back, up_ref[0])
    back += dot(mark, router_ref[:, :LANES], NT)
    back_ref[...] = back.reshape(back_ref.shape).astype(BF)
    part = dot(mark, x, TN)

    @pl.when(expert == 0)
    def _():
        route_ref[...] = jnp.zeros_like(route_ref)

    route_ref[...] += part


def chunk_spec(array, chunk):
    sources, _, _, slots, width = array.shape
    return pl.BlockSpec((sources, 1, 1, slots, width), lambda e: (0, chunk, e, 0, 0))


def expert_chunk(base, x_at, g_at, other, gate_w, up_w, down_w, router_pair, after):
    (x, x_chunk), (g, g_chunk) = x_at, g_at
    sources, _, here, slots, width = x.shape
    hidden = down_w.shape[1]
    count = sources * slots
    rows = pl.BlockSpec((sources, 1, slots, width), lambda e: (0, e, 0, 0))
    middle = pl.BlockSpec((1, count, hidden), lambda e: (e, 0, 0))
    weights = pl.BlockSpec((1, hidden, width), lambda e: (e, 0, 0))
    return launch(
        expert_kernel,
        (base, x, g, other, gate_w, up_w, down_w, router_pair),
        after,
        grid=(here,),
        in_specs=[
            pl.BlockSpec(memory_space=pltpu.SMEM),
            chunk_spec(x, x_chunk),
            chunk_spec(g, g_chunk),
            pl.BlockSpec((1, count, 1), lambda e: (e, 0, 0)),
            weights,
            weights,
            weights,
            pl.BlockSpec((width, 2 * LANES), lambda e: (0, 0)),
        ],
        out_specs=[rows, rows, middle, middle, middle, pl.BlockSpec((LANES, width), lambda e: (0, 0))],
        out_shape=[jax.ShapeDtypeStruct((sources, here, slots, width), BF)] * 2
        + [jax.ShapeDtypeStruct((here, count, hidden), BF)] * 3
        + [jax.ShapeDtypeStruct((LANES, width), F32)],
        name="experts",
        flops=12 * here * count * width * hidden * 2,
    )


def weight_kernel(*refs, chunks):
    xs, gs, hidden, gates, ups = (refs[i * chunks : (i + 1) * chunks] for i in range(5))
    gate_ref, up_ref, down_ref = refs[5 * chunks :]
    x = jnp.concatenate([flat(ref) for ref in xs], 0)
    gate_ref[0] = dot(jnp.concatenate([ref[0] for ref in gates], 0), x, TN)
    up_ref[0] = dot(jnp.concatenate([ref[0] for ref in ups], 0), x, TN)
    g = jnp.concatenate([flat(ref) for ref in gs], 0)
    down_ref[0] = dot(jnp.concatenate([ref[0] for ref in hidden], 0), g, TN)


def weight_grads(xs, gs, hidden, gates, ups, after):
    sources, _, here, slots, width = xs[0][0].shape
    depth = hidden[0].shape[2]
    middle = pl.BlockSpec((1, sources * slots, depth), lambda e: (e, 0, 0))
    chunks = len(xs)
    return launch(
        functools.partial(weight_kernel, chunks=chunks),
        (*[v for v, _ in xs], *[v for v, _ in gs], *hidden, *gates, *ups),
        after,
        grid=(here,),
        in_specs=[chunk_spec(*v) for v in (*xs, *gs)] + [middle] * (3 * chunks),
        out_specs=[pl.BlockSpec((1, depth, width), lambda e: (e, 0, 0))] * 3,
        out_shape=[jax.ShapeDtypeStruct((here, depth, width), F32)] * 3,
        name="expert_weight_grads",
        flops=4 * here * chunks * sources * slots * width * depth * 2,
    )


def body(
    n_expert,
    n_tensor,
    inputs,
    gain_one,
    w_query,
    w_key,
    w_value,
    w_out,
    rel_table,
    gain_two,
    router,
    w_gate,
    w_up,
    w_down,
    routes,
    buckets,
    grad_out,
):
    rows, width = inputs.shape
    experts = router.shape[1]
    here = w_gate.shape[0]
    tokens = routes.shape[0]
    cap = (5 * rows * TOP + 4 * experts - 1) // (4 * experts)
    slots = experts * cap
    seq = buckets.shape[0]
    share = seq // rows
    count = rel_table.shape[0]
    head_cols = w_query.shape[1]
    at_expert = lax.axis_index("expert")
    at_tensor = lax.axis_index("tensor")
    steps = range(n_tensor)
    far = range(2, n_tensor)
    last = [None]

    def swap(value, step):
        return lax.ppermute(value, "tensor", [(i, i ^ step) for i in range(n_tensor)])

    def exchange(value):
        return lax.all_to_all(value, "expert", split_axis=0, concat_axis=0, tiled=True)

    def ordered(run, *operands, after=()):
        before = last[0] if isinstance(last[0], tuple) else (last[0],)
        result = run(*operands, (*before, *after))
        last[0] = result[0] if isinstance(result, (list, tuple)) else result
        return result

    labels = jnp.arange(experts, dtype=jnp.int32)
    grouped = routes.T.reshape(TOP, n_expert * n_tensor, rows)
    marks = (grouped[:, :, None, :] == labels[:, None]).astype(BF)
    order = jnp.arange(rows, dtype=jnp.int32)
    earlier = (order[:, None] < order[None, :]).astype(BF)
    ahead = jnp.einsum("kges,st->kget", marks, earlier, preferred_element_type=F32)
    first_count = jnp.sum(marks[0].astype(F32), axis=-1, keepdims=True)
    ahead = ahead + jnp.stack([jnp.zeros_like(first_count), first_count])
    places = jnp.sum(ahead * marks.astype(F32), axis=2).astype(jnp.int32)
    slot_ids = jnp.where(places < cap, grouped * cap + places, -1)
    slot_ids = slot_ids.reshape(TOP, n_expert, n_tensor, rows)
    choices = grouped.reshape(TOP, n_expert, n_tensor, rows)

    def relative(value, axis):
        return jnp.stack([lax.dynamic_index_in_dim(value, at_tensor ^ i, axis, keepdims=False) for i in steps])

    own_ids = relative(lax.dynamic_index_in_dim(slot_ids, at_expert, 1, keepdims=False), 1)
    id_rows = [own_ids[i] for i in steps]
    id_cols = jnp.swapaxes(own_ids, 1, 2)
    local = slot_ids - at_expert * (here * cap)
    slot_here = jnp.arange(here * cap, dtype=jnp.int32)[:, None]
    partner = jnp.sum(
        jnp.where(local[0][:, :, None, :] == slot_here, choices[1][:, :, None, :], 0)
        + jnp.where(local[1][:, :, None, :] == slot_here, choices[0][:, :, None, :], 0),
        axis=-1,
    ).reshape(n_expert, n_tensor, here, cap)
    partners = jnp.swapaxes(relative(partner, 1), 1, 2).reshape(n_tensor, here, n_expert * cap, 1)

    def send(step, value, after=()):
        buffer = ordered(to_slots, id_rows[step], value, slots, after=after)
        return exchange(buffer.reshape(n_expert, here, cap, width))

    def home(step, value, more=(), kind=BF, after=()):
        return ordered(to_tokens, id_cols[step], value.reshape(slots, width), more, kind, after=after)

    def gather(value):
        whole = lax.all_gather(value, "tensor", axis=0, tiled=True).reshape(n_tensor, rows, width)
        return [lax.dynamic_index_in_dim(whole, at_tensor ^ i, 0, keepdims=False) for i in steps]

    def everywhere(values):
        total = jnp.concatenate([value.reshape(-1) for value in values])
        for axis, size in (("expert", n_expert), ("tensor", n_tensor)):
            for bit in range(size.bit_length() - 1):
                total = total + lax.ppermute(total, axis, [(i, i ^ (1 << bit)) for i in range(size)])
        totals = []
        for value in values:
            totals.append(total[: value.size].reshape(value.shape))
            total = total[value.size :]
        return totals

    def whole_seq(value):
        if share == 1:
            return value
        groups = [[i * share + j for j in range(share)] for i in range(n_tensor // share)]
        return lax.all_gather(value, "tensor", axis=0, tiled=True, axis_index_groups=groups)

    def own_rows(value):
        if share == 1:
            return value
        return lax.dynamic_slice_in_dim(value, (at_tensor % share) * rows, rows, 0)

    packed = jnp.concatenate([w_query.T, w_key.T, w_value.T, w_out], 0)
    strip = 4 * head_cols // n_expert
    blocks = 4 * head_cols // LANES
    pairs = blocks // 4
    own_w = packed.reshape(4, pairs, 1, LANES, width)
    packed = ordered(hold, lax.dynamic_slice_in_dim(packed, at_expert * strip, strip, 0))
    strips = jnp.stack([swap(packed, i) for i in steps[1:]])
    table_own = jnp.pad(rel_table.T, ((0, 0), (0, LANES - count)))
    table_all = jnp.stack([table_own] + [swap(table_own, i) for i in steps[1:]])
    table_all = table_all.reshape(n_tensor * pairs, 2, LANES)

    inputs_f = inputs.astype(F32)
    normed_one = rms_scale(inputs_f, gain_one).astype(BF)
    attn_in = whole_seq(normed_one)
    grad_low = ordered(hold, grad_out, after=(strips, table_all))
    grad_all = lax.all_gather(grad_low, "tensor", axis=0, tiled=True).reshape(n_tensor, rows, width)
    own_part = ordered(attend, attn_in, own_w, buckets, table_all[:pairs])

    bits = [1 << i for i in range(1, n_expert.bit_length() - 1)]
    sources = jnp.arange(n_expert, dtype=jnp.int32) ^ at_expert
    halves, places, came = [], [], []
    for half in range(2):
        held, order = strips[None, :, :, half * width // 2 : (half + 1) * width // 2], [0]
        for bit in (bits if half == 0 else bits[::-1]) + [1]:
            came.append(held)
            held = jnp.concatenate([held, lax.ppermute(held, "expert", [(i, i ^ bit) for i in range(n_expert)])], 0)
            order = order + [i ^ bit for i in order]
        halves.append(held)
        where = jnp.asarray([order.index(i) for i in range(n_expert)], jnp.int32)
        places.append(jnp.sum(jnp.where(sources[:, None] == jnp.arange(n_expert), where, 0), 1))
    places = jnp.stack(places).astype(jnp.int32)

    grad_own = send(0, grad_out, (came[len(bits)], came[-1]))
    attn_w = ordered(assemble, places, halves)
    others = jnp.arange(1, n_tensor, dtype=jnp.int32) ^ at_tensor
    grad_rest = exchange(
        ordered(to_many_slots, others, own_ids[1:], grad_all, (n_expert, here * cap), after=(grad_own,))
    )
    grad_slots = {0: (grad_own, 0)} | {i: (grad_rest, i - 1) for i in steps[1:]}
    attn_w = attn_w.reshape(blocks, n_expert // blocks, n_tensor - 1, strip, width)
    attn_w = jnp.swapaxes(attn_w, 1, 2).reshape(4, pairs, n_tensor - 1, LANES, width)
    rest_part = ordered(attend, attn_in, attn_w, buckets, table_all[pairs:])
    resid = inputs_f + own_rows(own_part[3] + rest_part[3])
    normed_two = rms_scale(resid, gain_two)
    normed_low = normed_two.astype(BF)

    token_far = gather(normed_low)
    token_slots = {0: send(0, normed_low, (grad_rest,))}

    counts = jnp.sum((routes.T[:, None, :] == labels[:, None]).astype(F32), axis=(0, 2))
    route_share = counts / (tokens * TOP)

    def losses(normed, router_w):
        logits = jnp.dot(normed, router_w, precision=highest)
        router_probs = jax.nn.softmax(logits, axis=-1)
        log_totals = jax.nn.logsumexp(logits, axis=-1)
        balance = experts * jnp.sum(route_share * jnp.sum(router_probs, axis=0)) / tokens
        return balance, jnp.sum(log_totals * log_totals) / tokens

    (balance_part, zloss_part), losses_back = jax.vjp(losses, normed_two, router)
    normed_grad, router_grad = losses_back(
        (jnp.asarray(balance_weight, F32), jnp.asarray(zloss_weight, F32))
    )

    router_high = router.astype(BF)
    router_low = (router - router_high.astype(F32)).astype(BF)
    fill = ((0, 0), (0, LANES - experts))
    router_pair = jnp.concatenate([jnp.pad(router_high, fill), jnp.pad(router_low, fill)], 1)
    base = jnp.full((1,), at_expert * here, jnp.int32)
    gate_w = jnp.swapaxes(w_gate, 1, 2)
    up_w = jnp.swapaxes(w_up, 1, 2)

    def rows_in(value):
        value, chunk = value
        if cap % 8 == 0:
            return value.reshape(n_expert, -1, here, cap, width), chunk
        value = value.reshape(n_expert, -1, here, cap, width)[:, chunk]
        return jnp.swapaxes(value, 0, 1).reshape(1, 1, here, n_expert * cap, width), 0

    def rows_out(value):
        if cap % 8 == 0:
            return value
        return jnp.swapaxes(value.reshape(here, n_expert, cap, width), 0, 1)

    xs, gs, done = {}, {}, {}

    def work(step):
        xs[step], gs[step] = rows_in((token_slots[step], 0)), rows_in(grad_slots[step])
        done[step] = ordered(
            expert_chunk, base, xs[step], gs[step], partners[step], gate_w, up_w, w_down, router_pair
        )

    token_slots[1] = send(1, token_far[1])
    work(0)
    for i in far:
        token_slots[i] = send(i, token_far[i])
        work(i - 1)
    work(n_tensor - 1)
    backs = {i: rows_out(done[i][1]) for i in steps}
    outs = {i: rows_out(done[i][0]) for i in steps}
    moe_far, near = [], None
    for i in far:
        moe_far.append(swap(home(i, exchange(backs[i]), after=moe_far[-1:]), i))
        if i == far[0]:
            near = exchange(ordered(add, backs[0], swap(backs[1], 1)))
    gate_grad, up_grad, down_grad = ordered(
        weight_grads,
        *[[v[i] for i in steps] for v in (xs, gs)],
        *[[done[i][j] for i in steps] for j in (2, 3, 4)],
    )
    moe_grad = home(0, near, moe_far, F32)
    router_grad = router_grad + sum(done[i][5] for i in steps)[:experts].T

    grad_f = grad_out.astype(F32)
    resid_norm_grad, gain_two_grad = jax.vjp(rms_scale, resid, gain_two)[1](normed_grad + moe_grad)
    resid_grad = grad_f + resid_norm_grad
    attn_grad = whole_seq(resid_grad.astype(BF))
    out_all = ordered(stack, jnp.arange(n_tensor, dtype=jnp.int32) ^ at_tensor, [outs[i] for i in steps])
    rest_back = ordered(attend_back, attn_in, attn_grad, attn_w, *rest_part[:3])
    own_back = ordered(attend_back, attn_in, attn_grad, own_w, *own_part[:3])
    out_sum = lax.psum_scatter(out_all, "tensor", scatter_dimension=0, tiled=True)
    out_sum = exchange(out_sum.reshape(n_expert, here, cap, width))
    normed_one_grad = own_back[2] + rest_back[2]

    side = at_expert % 2

    def pair_sum(weight_parts):
        groups = weight_parts.shape[2]
        parts = weight_parts.reshape(blocks, groups, n_expert // blocks, strip, width)
        parts = jnp.swapaxes(parts, 1, 2).reshape(n_expert // 2, 2, groups, strip, width)
        kept = lax.dynamic_index_in_dim(parts, side, 1, keepdims=False)
        given = lax.dynamic_index_in_dim(parts, 1 - side, 1, keepdims=False)
        given = lax.ppermute(given, "expert", [(i, i ^ 1) for i in range(n_expert)])
        return (kept.astype(F32) + given.astype(F32)).astype(BF)

    def plane_sum(parts):
        parts = lax.all_to_all(
            parts,
            "expert",
            split_axis=0,
            concat_axis=0,
            tiled=True,
            axis_index_groups=[list(range(i, n_expert, 2)) for i in range(2)],
        )
        return jnp.sum(parts.astype(F32), axis=0).astype(BF)

    parts = [pair_sum(own_back[0]), pair_sum(rest_back[0])]
    parts = [plane_sum(part) for part in parts]
    parts = [part[i] for part in parts for i in range(part.shape[0])]
    table_grad = ordered(table_back, (own_back[1], rest_back[1]), buckets, count)
    input_norm_grad, gain_one_grad = jax.vjp(rms_scale, inputs_f, gain_one)[1](own_rows(normed_one_grad))
    input_grad = resid_grad + input_norm_grad

    table_grad = relative(table_grad.T.reshape(n_tensor, rel_table.shape[1], count), 0) / share
    small = [router_grad.T, gain_one_grad, gain_two_grad, table_grad, jnp.stack([balance_part, zloss_part])]
    router_total, gain_one_total, gain_two_total, table_total, loss_total = everywhere(small)
    strip_grad = ordered(add, parts[0], *[swap(parts[i], i) for i in steps[1:]], after=(gain_one_total,))
    if share > 1:
        strip_grad = (strip_grad.astype(F32) / share).astype(BF)
    output = home(0, out_sum, (resid,), BF)

    attn_w_grad = lax.all_gather(strip_grad, "expert", axis=0, tiled=True)
    query_grad, key_grad, value_grad, out_proj_grad = ordered(split, attn_w_grad)
    table_total = lax.dynamic_index_in_dim(table_total, at_tensor, 0, keepdims=False).T
    return (
        output,
        input_grad,
        gain_one_total,
        query_grad,
        key_grad,
        value_grad,
        out_proj_grad,
        table_total,
        gain_two_total,
        router_total.T,
        jnp.swapaxes(gate_grad, 1, 2),
        jnp.swapaxes(up_grad, 1, 2),
        down_grad,
        loss_total,
    )


def solution(mesh):
    return jax.shard_map(
        functools.partial(body, mesh.shape["expert"], mesh.shape["tensor"]),
        mesh=mesh,
        in_specs=(
            P(("expert", "tensor"), None),
            P(),
            P(None, "tensor"),
            P(None, "tensor"),
            P(None, "tensor"),
            P("tensor", None),
            P(None, "tensor"),
            P(),
            P(),
            P("expert", None, "tensor"),
            P("expert", None, "tensor"),
            P("expert", "tensor", None),
            P(),
            P(),
            P(("expert", "tensor"), None),
        ),
        out_specs=(
            P(("expert", "tensor"), None),
            P(("expert", "tensor"), None),
            P(),
            P(None, "tensor"),
            P(None, "tensor"),
            P(None, "tensor"),
            P("tensor", None),
            P(None, "tensor"),
            P(),
            P(),
            P("expert", None, "tensor"),
            P("expert", None, "tensor"),
            P("expert", "tensor", None),
            P(),
        ),
        check_vma=False,
    )
```
